32 devices in a mesh: hist: 16 (over z, y, core), col: 2 (over x).
Axes of the slice: x: 2, y: 2, z: 4, core: 2. Of those that a mesh axis runs over, the one named last changes fastest.
Arguments:
- lesser: float32 [16, 128, 16, 128], P('col', None, 'hist'), may hold values from -0.1875 to 0.1875
- advanced: float32 [16, 128, 16, 128], P('col', None, 'hist'), may hold values from -0.1875 to 0.1875
- first_row: float32 [128, 16, 128], P(None, 'col'), may hold values from -4 to 4
- greater_rows: float32 [4, 128, 16, 128], P(None, None, 'col'), may hold values from -4 to 4
- hamiltonian: float32 [128, 128], replicated, may hold values from -0.5 to 0.5
- coupling: float32 [128, 128], replicated, may hold values from 0.3 to 1
- cutoff: int32 [16], P('hist'), may hold values from 1 to 16, as said below
- step_index: int32 [1], replicated, may hold values from 4 to 11
Outputs:
- final_row: float32 [128, 16, 128], P(None, 'col')
The draws below stay inside these ranges and needn't reach their ends.
Inputs may be any that keep to these rules, and one draw needn't show every extreme that they name: Some second time has cutoff 16.
All inputs are finite; a program needn't handle non-finite values.
Results may differ from the reference program's by a relative error of at most 0.0001.
Values sent between devices are 32-bit elements; how exact they have to be, the bound alone decides.
No kernel may reach another device: no remote copies, remote signals or barrier semaphores. Data moves between devices by JAX's collectives and lax.ppermute only.
A program may use at most 64 MiB of HBM per device.

```python
import math
import jax
import jax.numpy as jnp
from jax import lax

NORB = 128
STEPS = 4
TIMES = 16


def draw_cutoff(key, part):
    drawn = jax.random.randint(jax.random.fold_in(key, 11), (TIMES,), 1, TIMES + 1)
    chosen = jax.random.randint(jax.random.fold_in(key, 12), (), 0, TIMES)
    return jnp.where(jnp.arange(TIMES) == chosen, TIMES, drawn).astype(jnp.int32)


def raised(result, key, source, target, shards_of, factor):
    def block_of(axis_at):
        return (jnp.arange(result.shape[axis_at]) // (result.shape[axis_at] // shards_of)).reshape((-1,) + (1,) * (result.ndim - 1 - axis_at))

    one_side = jax.random.permutation(key, shards_of)[block_of(target)]
    other_side = (block_of(target) + shards_of // 2) % shards_of
    return jnp.where((block_of(source) == one_side) | (block_of(source) == other_side), factor * result, result)


def steps_of(own_key, shape, cuts, least, high):
    level, own = 1.0, jax.random.fold_in(own_key, 6)
    for position, blocks in cuts:
        steps = jnp.exp(jax.random.uniform(jax.random.fold_in(own, position), (blocks,), jnp.float32, least / len(cuts), high / len(cuts)))
        level = level * jnp.repeat(steps, shape[position] // blocks).reshape([-1 if axis == position else 1 for axis in range(len(shape))])
    return level


def centred(key, dims, deviation, bound, split=(), kind=jnp.bfloat16):
    array = jax.random.normal(key, dims, jnp.float32) * deviation
    if len(split) > 0:
        array = steps_of(key, dims, split, -0.22, 0.18) * array
    return jnp.clip(array, min=-bound, max=bound).astype(kind)


def heavy_noise(key, dims, deviation, bound, shards, heavy, kind=jnp.bfloat16):
    values = deviation * jax.random.normal(key, dims, jnp.float32)
    if shards:
        values = values * steps_of(key, dims, shards, -0.22, 0.18)
    return jnp.clip(raised(values, jax.random.fold_in(key, 3), *heavy), -bound, bound).astype(kind)


def setup_inputs(seed: int = 0) -> dict:
    keys = jax.random.split(jax.random.key(seed), 9)
    return {
        "lesser": heavy_noise(keys[0], (TIMES, NORB, TIMES, NORB), (TIMES * NORB) ** -0.5, 0.1875, ((0, 2), (2, 16)), (0, 2, 16, 2.0), jnp.float32),
        "advanced": heavy_noise(keys[1], (TIMES, NORB, TIMES, NORB), (TIMES * NORB) ** -0.5, 0.1875, ((0, 2), (2, 16)), (0, 2, 16, 2.0), jnp.float32),
        "first_row": centred(keys[2], (NORB, TIMES, NORB), 1.0, 4.0, ((1, 2),), jnp.float32),
        "greater_rows": centred(keys[3], (STEPS, NORB, TIMES, NORB), 1.0, 4.0, ((2, 2),), jnp.float32),
        "hamiltonian": centred(keys[4], (NORB, NORB), NORB ** -0.5, 0.5, (), jnp.float32),
        "coupling": jnp.clip(jnp.exp(jax.random.uniform(keys[5], (NORB, NORB), jnp.float32, math.log(0.3), math.log(1.0))), 0.3, 1.0),
        "cutoff": draw_cutoff(jax.random.fold_in(keys[8], 71), 0),
        "step_index": jax.random.randint(keys[7], (1,), TIMES // 4, 3 * TIMES // 4).astype(jnp.int32),
    }


STEP_SIZE = 0.2
PRECISE = lax.Precision.HIGHEST


def reference(lesser, advanced, first_row, greater_rows, hamiltonian, coupling, cutoff, step_index):
    times = lesser.shape[0]
    orbitals = lesser.shape[1]
    positions = jnp.arange(times, dtype=jnp.int32)
    inside = (positions[:, None] < cutoff[None, :]).astype(jnp.float32)
    adv_flat = (advanced * inside[:, None, :, None]).reshape(times * orbitals, times * orbitals)
    hist_flat = lesser.reshape(times * orbitals, times * orbitals)
    propagator = jnp.eye(orbitals, dtype=jnp.float32) - STEP_SIZE * hamiltonian
    strength = (coupling * coupling)[:, None, :]
    current = first_row
    for section in range(STEPS):
        greater = greater_rows[section]
        sigma_less = -strength * current * current * greater
        sigma_ret = -strength * greater * greater * current - sigma_less
        active = (positions < step_index[0] + section).astype(jnp.float32)
        sigma_ret = sigma_ret * active[None, :, None]
        memory = jnp.dot(sigma_ret.reshape(orbitals, times * orbitals), hist_flat, precision=PRECISE, preferred_element_type=jnp.float32)
        memory = memory + jnp.dot(sigma_less.reshape(orbitals, times * orbitals), adv_flat, precision=PRECISE, preferred_element_type=jnp.float32)
        moved = jnp.einsum("ik,ksj->isj", propagator, current, precision=PRECISE)
        current = moved - STEP_SIZE * memory.reshape(orbitals, times, orbitals)
    return current
```

```python
import functools

import jax
import jax.numpy as jnp
from jax import lax
from jax.experimental import pallas as pl
from jax.experimental.pallas import tpu as pltpu
from jax.sharding import PartitionSpec as P

STEP_SIZE = 0.2
BF16 = jnp.bfloat16
F32 = jnp.float32


def split(x):
    high = x.astype(BF16)
    return high, (x - high.astype(F32)).astype(BF16)


def times_wide(high, low, wide):
    n = wide.shape[-1] // 2
    first = jnp.dot(high, wide, preferred_element_type=F32)
    second = jnp.dot(low, wide[:, :n], preferred_element_type=F32)
    return first[:, :n] + first[:, n:] + second


def advance(section, rows_dev, n, owner, own_row, cur, g_ref, coup_ref, ham_ref, active_ref, wide_ref, part_ref, high_ref, low_ref):
    coup = coup_ref[...]
    strength = coup * coup
    for s in range(rows_dev):
        x = cur[s]
        g = g_ref[pl.ds(s, n, stride=rows_dev), :]
        active = active_ref[pl.ds(section * rows_dev + s, 1), :]
        u = strength * x * g
        less = -(u * x)
        ret = (u * x - u * g) * active
        for where, value in ((s, ret), (rows_dev + s, less)):
            high, low = split(value)
            high_ref[:, where * n : (where + 1) * n] = high
            low_ref[:, where * n : (where + 1) * n] = low
    total = times_wide(high_ref[...], low_ref[...], wide_ref[...])
    h_high, h_low = split(ham_ref[...])
    row = cur[own_row] * owner
    row_wide = jnp.concatenate(split(row), axis=1)
    part_ref[...] = total + times_wide(h_high, h_low, row_wide)


def places(rows_dev):
    hist_pos, col_pos = lax.axis_index("hist"), lax.axis_index("col")
    own_row = lax.rem(hist_pos, rows_dev)
    owner = jnp.where(lax.div(hist_pos, rows_dev) == col_pos, 1.0, 0.0).astype(F32)
    return own_row, owner, col_pos


def first_kernel(rows_dev, n, steps, step_ref, cutoff_ref, lesser_ref, adv_ref, first_ref, g_ref, coup_ref, ham_ref,
                 cur_ref, wide_ref, active_ref, part_ref, high_ref, low_ref):
    own_row, owner, col_pos = places(rows_dev)
    cutoff, start = cutoff_ref[0], step_ref[0]
    for s in range(rows_dev):
        time = col_pos * rows_dev + s
        cur_ref[s] = first_ref[pl.ds(s, n, stride=rows_dev), :]
        for q in range(steps):
            active_ref[q * rows_dev + s : q * rows_dev + s + 1, :] = jnp.full(
                (1, n), jnp.where(time < start + q, 1.0, 0.0).astype(F32)
            )
        inside = jnp.where(time < cutoff, 1.0, 0.0).astype(F32)
        for where, value in (
            (s, lesser_ref[s * n : (s + 1) * n, :]),
            (rows_dev + s, adv_ref[s * n : (s + 1) * n, :] * inside),
        ):
            high, low = split(value)
            wide_ref[where * n : (where + 1) * n, :n] = high
            wide_ref[where * n : (where + 1) * n, n:] = low
    advance(0, rows_dev, n, owner, own_row, cur_ref, g_ref, coup_ref, ham_ref, active_ref, wide_ref, part_ref, high_ref, low_ref)


def next_kernel(section, rows_dev, n, order, prev_ref, g_ref, coup_ref, ham_ref, active_ref, wide_ref, *rest):
    pieces, (cur_ref, part_ref, high_ref, low_ref) = rest[:rows_dev], rest[rows_dev:]
    own_row, owner, _ = places(rows_dev)
    for k, piece in enumerate(pieces):
        s = order(own_row, k)
        cur_ref[s] = prev_ref[s] - STEP_SIZE * piece[...]
    advance(section, rows_dev, n, owner, own_row, cur_ref, g_ref, coup_ref, ham_ref, active_ref, wide_ref, part_ref, high_ref, low_ref)


def last_kernel(rows_dev, n, order, prev_ref, *rest):
    pieces, (out_ref,) = rest[:rows_dev], rest[rows_dev:]
    own_row, _, _ = places(rows_dev)
    for k, piece in enumerate(pieces):
        s = order(own_row, k)
        out_ref[pl.ds(s, n, stride=rows_dev), :] = prev_ref[s] - STEP_SIZE * piece[...]


def call(kernel, outs, scratch, smem, vmem, name):
    return pl.pallas_call(
        kernel,
        out_shape=outs,
        in_specs=[pl.BlockSpec(memory_space=pltpu.SMEM)] * smem + [pl.BlockSpec(memory_space=pltpu.VMEM)] * vmem,
        out_specs=jax.tree.map(lambda _: pl.BlockSpec(memory_space=pltpu.VMEM), outs),
        scratch_shapes=scratch,
        name=name,
    )


def exchange_pairs(hist, rows_dev, part):
    def at(h, c):
        return h * 2 + c

    def moved(x, pairs):
        return lax.ppermute(x, ("hist", "col"), pairs)

    def flip(x, bits):
        return moved(x, [(at(h, c), at(h ^ bits, c)) for h in range(hist) for c in range(2)])

    total = part + moved(part, [(at(h, c), at(h, 1 - c)) for h in range(hist) for c in range(2)])
    other = flip(total, rows_dev)
    reads_own = lax.axis_index("hist") // rows_dev == lax.axis_index("col")
    own = jnp.where(reads_own, total, other)
    pieces = [own] + [None] * (rows_dev - 1)
    for bits in range(2, rows_dev, 2):
        pieces[bits] = flip(own, bits)
    for bits in range(0, rows_dev, 2):
        pieces[bits + 1] = flip(pieces[bits], 1)
    return pieces


def exchange_any(rows_dev, part):
    total = lax.psum(part, "col")
    rows = lax.all_gather(total, "hist", axis=0)
    block = lax.dynamic_slice_in_dim(rows, lax.axis_index("col") * rows_dev, rows_dev, axis=0)
    return [block[s] for s in range(rows_dev)]


def on_device(hist, cols, lesser, advanced, first_row, greater_rows, hamiltonian, coupling, cutoff, step_index):
    rows_dev, n, cols_dev, _ = lesser.shape
    steps = greater_rows.shape[0]
    assert cols_dev == 1 and hist == cols * rows_dev
    flat = (rows_dev * n, n)
    pairs = cols == 2 and hist & (hist - 1) == 0 and rows_dev >= 2
    if pairs:
        exchange = functools.partial(exchange_pairs, hist, rows_dev)
        order = lambda own_row, k: jnp.bitwise_xor(own_row, k)
    else:
        exchange = functools.partial(exchange_any, rows_dev)
        order = lambda own_row, k: k
    shape = jax.ShapeDtypeStruct
    cur_shape, part_shape = shape((rows_dev, n, n), F32), shape((n, n), F32)
    scratch = [pltpu.VMEM((n, 2 * rows_dev * n), BF16)] * 2
    current, wide, active, part = call(
        functools.partial(first_kernel, rows_dev, n, steps),
        (cur_shape, shape((2 * rows_dev * n, 2 * n), BF16), shape((steps * rows_dev, n), F32), part_shape),
        scratch, 2, 6, "first_step",
    )(step_index, cutoff, lesser.reshape(flat), advanced.reshape(flat), first_row.reshape(flat),
      greater_rows[0].reshape(flat), coupling, hamiltonian)
    for section in range(1, steps):
        pieces = exchange(part)
        current, part = call(
            functools.partial(next_kernel, section, rows_dev, n, order),
            (cur_shape, part_shape), scratch, 0, 6 + rows_dev, "next_step",
        )(current, greater_rows[section].reshape(flat), coupling, hamiltonian, active, wide, *pieces)
    pieces = exchange(part)
    final = call(
        functools.partial(last_kernel, rows_dev, n, order), shape(flat, F32), [], 0, 1 + rows_dev, "last_step",
    )(current, *pieces)
    return final.reshape(first_row.shape)


def solution(mesh):
    in_specs = (
        P("col", None, "hist", None),
        P("col", None, "hist", None),
        P(None, "col", None),
        P(None, None, "col", None),
        P(),
        P(),
        P("hist"),
        P(),
    )
    return jax.shard_map(
        functools.partial(on_device, mesh.shape["hist"], mesh.shape["col"]),
        mesh=mesh, in_specs=in_specs, out_specs=P(None, "col", None), check_vma=False,
    )
```

```python
import functools

import jax
import jax.numpy as jnp
from jax import lax
from jax.experimental import pallas as pl
from jax.experimental.pallas import tpu as pltpu
from jax.sharding import PartitionSpec as P

STEP_SIZE = 0.2
BF16 = jnp.bfloat16
F32 = jnp.float32
VMEM_BYTES = 12 * 2**20


def split(x):
    high = x.astype(BF16)
    return high, (x - high.astype(F32)).astype(BF16)


def times_wide(high, low, wide):
    n = wide.shape[-1] // 2
    first = jnp.dot(high, wide, preferred_element_type=F32)
    second = jnp.dot(low, wide[:, :n], preferred_element_type=F32)
    return first[:, :n] + first[:, n:] + second


def advance(section, rows_dev, n, owner, own_row, cur, g_ref, coup_ref, ham_ref, active_ref, wide_ref, part_ref, high_ref, low_ref):
    coup = coup_ref[...]
    strength = coup * coup
    for s in range(rows_dev):
        x = cur[s]
        g = g_ref[pl.ds(section * rows_dev * n + s, n, stride=rows_dev), :]
        active = active_ref[pl.ds(section * rows_dev + s, 1), :]
        u = strength * x * g
        less = -(u * x)
        ret = (u * x - u * g) * active
        for where, value in ((s, ret), (rows_dev + s, less)):
            high, low = split(value)
            high_ref[:, where * n : (where + 1) * n] = high
            low_ref[:, where * n : (where + 1) * n] = low
    total = times_wide(high_ref[...], low_ref[...], wide_ref[...])
    h_high, h_low = split(ham_ref[...])
    row = cur[own_row] * owner
    row_wide = jnp.concatenate(split(row), axis=1)
    part_ref[...] = total + times_wide(h_high, h_low, row_wide)


def places(rows_dev):
    hist_pos, col_pos = lax.axis_index("hist"), lax.axis_index("col")
    own_row = lax.rem(hist_pos, rows_dev)
    owner = jnp.where(lax.div(hist_pos, rows_dev) == col_pos, 1.0, 0.0).astype(F32)
    return own_row, owner, col_pos


def first_kernel(rows_dev, n, steps, step_ref, cutoff_ref, lesser_ref, adv_ref, first_ref, g_ref, coup_ref, ham_ref,
                 cur_ref, wide_ref, active_ref, part_ref, high_ref, low_ref):
    own_row, owner, col_pos = places(rows_dev)
    cutoff, start = cutoff_ref[0], step_ref[0]
    for s in range(rows_dev):
        time = col_pos * rows_dev + s
        cur_ref[s] = first_ref[pl.ds(s, n, stride=rows_dev), :]
        for q in range(steps):
            active_ref[q * rows_dev + s : q * rows_dev + s + 1, :] = jnp.full(
                (1, n), jnp.where(time < start + q, 1.0, 0.0).astype(F32)
            )
        inside = jnp.where(time < cutoff, 1.0, 0.0).astype(F32)
        for where, value in (
            (s, lesser_ref[s * n : (s + 1) * n, :]),
            (rows_dev + s, adv_ref[s * n : (s + 1) * n, :] * inside),
        ):
            high, low = split(value)
            wide_ref[where * n : (where + 1) * n, :n] = high
            wide_ref[where * n : (where + 1) * n, n:] = low
    advance(0, rows_dev, n, owner, own_row, cur_ref, g_ref, coup_ref, ham_ref, active_ref, wide_ref, part_ref, high_ref, low_ref)


def next_kernel(section, rows_dev, n, order, prev_ref, g_ref, coup_ref, ham_ref, active_ref, wide_ref, *rest):
    pieces, (cur_ref, part_ref, high_ref, low_ref) = rest[:rows_dev], rest[rows_dev:]
    own_row, owner, _ = places(rows_dev)
    for k, piece in enumerate(pieces):
        s = order(own_row, k)
        cur_ref[s] = prev_ref[s] - STEP_SIZE * piece[...]
    advance(section, rows_dev, n, owner, own_row, cur_ref, g_ref, coup_ref, ham_ref, active_ref, wide_ref, part_ref, high_ref, low_ref)


def last_kernel(rows_dev, n, order, prev_ref, *rest):
    pieces, (out_ref,) = rest[:rows_dev], rest[rows_dev:]
    own_row, _, _ = places(rows_dev)
    for k, piece in enumerate(pieces):
        s = order(own_row, k)
        out_ref[pl.ds(s, n, stride=rows_dev), :] = prev_ref[s] - STEP_SIZE * piece[...]


def call(kernel, outs, scratch, smem, vmem, name):
    return pl.pallas_call(
        kernel,
        out_shape=outs,
        in_specs=[pl.BlockSpec(memory_space=pltpu.SMEM)] * smem + [pl.BlockSpec(memory_space=pltpu.VMEM)] * vmem,
        out_specs=jax.tree.map(lambda _: pl.BlockSpec(memory_space=pltpu.VMEM), outs),
        scratch_shapes=scratch,
        compiler_params=pltpu.CompilerParams(vmem_limit_bytes=VMEM_BYTES),
        name=name,
    )


def exchange_pairs(hist, rows_dev, part):
    def at(h, c):
        return h * 2 + c

    def moved(x, pairs):
        return lax.ppermute(x, ("hist", "col"), pairs)

    def flip(x, bits):
        return moved(x, [(at(h, c), at(h ^ bits, c)) for h in range(hist) for c in range(2)])

    total = part + moved(part, [(at(h, c), at(h, 1 - c)) for h in range(hist) for c in range(2)])
    other = flip(total, rows_dev)
    reads_own = lax.axis_index("hist") // rows_dev == lax.axis_index("col")
    own = jnp.where(reads_own, total, other)
    pieces = [own] + [None] * (rows_dev - 1)
    for bits in range(2, rows_dev, 2):
        pieces[bits] = flip(own, bits)
    for bits in range(0, rows_dev, 2):
        pieces[bits + 1] = flip(pieces[bits], 1)
    return pieces


def exchange_any(rows_dev, part):
    total = lax.psum(part, "col")
    rows = lax.all_gather(total, "hist", axis=0)
    block = lax.dynamic_slice_in_dim(rows, lax.axis_index("col") * rows_dev, rows_dev, axis=0)
    return [block[s] for s in range(rows_dev)]


def on_device(hist, cols, lesser, advanced, first_row, greater_rows, hamiltonian, coupling, cutoff, step_index):
    rows_dev, n, cols_dev, _ = lesser.shape
    steps = greater_rows.shape[0]
    assert cols_dev == 1 and hist == cols * rows_dev
    flat = (rows_dev * n, n)
    pairs = cols == 2 and hist & (hist - 1) == 0 and rows_dev >= 2
    if pairs:
        exchange = functools.partial(exchange_pairs, hist, rows_dev)
        order = lambda own_row, k: jnp.bitwise_xor(own_row, k)
    else:
        exchange = functools.partial(exchange_any, rows_dev)
        order = lambda own_row, k: k
    shape = jax.ShapeDtypeStruct
    cur_shape, part_shape = shape((rows_dev, n, n), F32), shape((n, n), F32)
    greater = greater_rows.reshape(steps * rows_dev * n, n)
    scratch = [pltpu.VMEM((n, 2 * rows_dev * n), BF16)] * 2
    current, wide, active, part = call(
        functools.partial(first_kernel, rows_dev, n, steps),
        (cur_shape, shape((2 * rows_dev * n, 2 * n), BF16), shape((steps * rows_dev, n), F32), part_shape),
        scratch, 2, 6, "first_step",
    )(step_index, cutoff, lesser.reshape(flat), advanced.reshape(flat), first_row.reshape(flat),
      greater, coupling, hamiltonian)
    for section in range(1, steps):
        pieces = exchange(part)
        current, part = call(
            functools.partial(next_kernel, section, rows_dev, n, order),
            (cur_shape, part_shape), scratch, 0, 6 + rows_dev, "next_step",
        )(current, greater, coupling, hamiltonian, active, wide, *pieces)
    pieces = exchange(part)
    final = call(
        functools.partial(last_kernel, rows_dev, n, order), shape(flat, F32), [], 0, 1 + rows_dev, "last_step",
    )(current, *pieces)
    return final.reshape(first_row.shape)


def solution(mesh):
    in_specs = (
        P("col", None, "hist", None),
        P("col", None, "hist", None),
        P(None, "col", None),
        P(None, None, "col", None),
        P(),
        P(),
        P("hist"),
        P(),
    )
    return jax.shard_map(
        functools.partial(on_device, mesh.shape["hist"], mesh.shape["col"]),
        mesh=mesh, in_specs=in_specs, out_specs=P(None, "col", None), check_vma=False,
    )
```

```python
import functools

import jax
import jax.numpy as jnp
from jax import lax
from jax.experimental import pallas as pl
from jax.experimental.pallas import tpu as pltpu
from jax.sharding import PartitionSpec as P

STEP_SIZE = 0.2
BF16 = jnp.bfloat16
F32 = jnp.float32
VMEM_BYTES = 12 * 2**20
PARTS = 4


def split(x):
    high = x.astype(BF16)
    return high, (x - high.astype(F32)).astype(BF16)


def times_wide(high, low, wide):
    n = wide.shape[-1] // 2
    first = jnp.dot(high, wide, preferred_element_type=F32)
    second = jnp.dot(low, wide[:, :n], preferred_element_type=F32)
    return first[:, :n] + first[:, n:] + second


def advance(section, rows_dev, n, owner, own_row, cur, g_ref, active_ref, strength_ref, ham_ref, wide_ref, part_ref, high_ref, low_ref):
    strength = strength_ref[...]
    for s in range(rows_dev):
        x = cur[s]
        g = g_ref[pl.ds(s, n, stride=rows_dev), :]
        active = active_ref[pl.ds(section * rows_dev + s, 1), :]
        u = strength * x * g
        less = -(u * x)
        ret = (u * x - u * g) * active
        for where, value in ((s, ret), (rows_dev + s, less)):
            high, low = split(value)
            high_ref[:, where * n : (where + 1) * n] = high
            low_ref[:, where * n : (where + 1) * n] = low
    total = times_wide(high_ref[...], low_ref[...], wide_ref[...])
    row = cur[own_row] * owner
    row_wide = jnp.concatenate(split(row), axis=1)
    part_ref[...] = total + times_wide(ham_ref[:, :n], ham_ref[:, n:], row_wide)


def places(rows_dev):
    hist_pos, col_pos = lax.axis_index("hist"), lax.axis_index("col")
    own_row = lax.rem(hist_pos, rows_dev)
    owner = jnp.where(lax.div(hist_pos, rows_dev) == col_pos, 1.0, 0.0).astype(F32)
    return own_row, owner, col_pos


def first_kernel(rows_dev, n, steps, step_hbm, cutoff_hbm, lesser_hbm, adv_hbm, first_hbm, g_hbm, coup_hbm, ham_hbm,
                 cur_ref, wide_ref, active_ref, strength_ref, ham_ref, part_ref,
                 high_ref, low_ref, step_ref, cutoff_ref, coup_ref, h_ref, first_ref, g_ref, table_ref, sems):
    sources = [(step_hbm, step_ref), (cutoff_hbm, cutoff_ref), (coup_hbm, coup_ref), (ham_hbm, h_ref)]
    half = rows_dev * n // PARTS
    for part in range(PARTS):
        rows = pl.ds(part * half, half)
        sources += [(first_hbm.at[rows], first_ref.at[rows]), (g_hbm.at[rows], g_ref.at[rows])]
    for table, source in enumerate((lesser_hbm, adv_hbm)):
        for part in range(PARTS):
            rows = pl.ds(part * half, half)
            sources.append((source.at[rows], table_ref.at[pl.ds(table * rows_dev * n + part * half, half)]))
    copies = [pltpu.make_async_copy(a, b, sems.at[k]) for k, (a, b) in enumerate(sources)]
    for copy in copies:
        copy.start()
    own_row, owner, col_pos = places(rows_dev)
    for copy in copies[:4]:
        copy.wait()
    cutoff, start = cutoff_ref[0], step_ref[0]
    coup = coup_ref[...]
    strength_ref[...] = coup * coup
    ham_ref[...] = jnp.concatenate(split(h_ref[...]), axis=1)
    for q in range(steps):
        for s in range(rows_dev):
            active_ref[q * rows_dev + s : q * rows_dev + s + 1, :] = jnp.full(
                (1, n), jnp.where(col_pos * rows_dev + s < start + q, 1.0, 0.0).astype(F32)
            )
    for copy in copies[4 : 4 + 2 * PARTS]:
        copy.wait()
    for s in range(rows_dev):
        cur_ref[s] = first_ref[pl.ds(s, n, stride=rows_dev), :]
    for table in range(2):
        for part in range(PARTS):
            copies[4 + (2 + table) * PARTS + part].wait()
            for s in range(part * rows_dev // PARTS, (part + 1) * rows_dev // PARTS):
                inside = jnp.where(col_pos * rows_dev + s < cutoff, 1.0, 0.0).astype(F32)
                where = (table * rows_dev + s) * n
                value = table_ref[where : where + n, :]
                wide_ref[where : where + n, :] = jnp.concatenate(split(value * inside if table else value), axis=1)
    advance(0, rows_dev, n, owner, own_row, cur_ref, g_ref, active_ref, strength_ref, ham_ref, wide_ref, part_ref, high_ref, low_ref)


def next_kernel(section, rows_dev, n, order, prev_ref, greater_ref, active_ref, strength_ref, ham_ref, wide_ref, *rest):
    pieces, (cur_ref, part_ref, high_ref, low_ref) = rest[:rows_dev], rest[rows_dev:]
    own_row, owner, _ = places(rows_dev)
    for k, piece in enumerate(pieces):
        s = order(own_row, k)
        cur_ref[s] = prev_ref[s] - STEP_SIZE * piece[...]
    g_ref = greater_ref.at[pl.ds(section * rows_dev * n, rows_dev * n)]
    advance(section, rows_dev, n, owner, own_row, cur_ref, g_ref, active_ref, strength_ref, ham_ref, wide_ref, part_ref, high_ref, low_ref)


def last_kernel(rows_dev, n, order, prev_ref, *rest):
    pieces, (out_hbm, out_ref, sems) = rest[:rows_dev], rest[rows_dev:]
    own_row, _, _ = places(rows_dev)
    size = n // PARTS
    copies = []
    for part in range(PARTS):
        rows = pl.ds(part * size, size)
        for k, piece in enumerate(pieces):
            s = order(own_row, k)
            out_ref[pl.ds(part * size * rows_dev + s, size, stride=rows_dev), :] = prev_ref[s, rows, :] - STEP_SIZE * piece[rows, :]
        flat = pl.ds(part * size * rows_dev, size * rows_dev)
        copies.append(pltpu.make_async_copy(out_ref.at[flat], out_hbm.at[flat], sems.at[part]))
        copies[-1].start()
    for copy in copies:
        copy.wait()


def call(kernel, ins, outs, scratch, name):
    return pl.pallas_call(
        kernel,
        out_shape=[shape for shape, _ in outs],
        in_specs=[pl.BlockSpec(memory_space=space) for space in ins],
        out_specs=[pl.BlockSpec(memory_space=space) for _, space in outs],
        scratch_shapes=scratch,
        compiler_params=pltpu.CompilerParams(vmem_limit_bytes=VMEM_BYTES),
        name=name,
    )


def exchange_pairs(hist, rows_dev, part):
    def at(h, c):
        return h * 2 + c

    def moved(x, pairs):
        return lax.ppermute(x, ("hist", "col"), pairs)

    def flip(x, bits):
        return moved(x, [(at(h, c), at(h ^ bits, c)) for h in range(hist) for c in range(2)])

    def block(h):
        return h // rows_dev

    cycle = [(at(h, 1 - block(h)), at(h, block(h))) for h in range(hist)]
    cycle += [(at(h, block(h)), at(h ^ rows_dev, block(h))) for h in range(hist)]
    across = [(at(h, 1 - block(h)), at(h ^ rows_dev, block(h))) for h in range(hist)]
    across += [(at(h, block(h)), at(h, block(h))) for h in range(hist)]
    own = moved(part, cycle) + moved(part, across)
    pieces = [own] + [None] * (rows_dev - 1)
    for bits in range(2, rows_dev, 2):
        pieces[bits] = flip(own, bits)
    for bits in range(0, rows_dev, 2):
        pieces[bits + 1] = flip(pieces[bits], 1)
    return pieces


def exchange_any(rows_dev, part):
    total = lax.psum(part, "col")
    rows = lax.all_gather(total, "hist", axis=0)
    block = lax.dynamic_slice_in_dim(rows, lax.axis_index("col") * rows_dev, rows_dev, axis=0)
    return [block[s] for s in range(rows_dev)]


def on_device(hist, cols, lesser, advanced, first_row, greater_rows, hamiltonian, coupling, cutoff, step_index):
    rows_dev, n, cols_dev, _ = lesser.shape
    steps = greater_rows.shape[0]
    assert cols_dev == 1 and hist == cols * rows_dev
    flat = (rows_dev * n, n)
    pairs = cols == 2 and hist & (hist - 1) == 0 and rows_dev >= 2
    if pairs:
        exchange = functools.partial(exchange_pairs, hist, rows_dev)
        order = lambda own_row, k: jnp.bitwise_xor(own_row, k)
    else:
        exchange = functools.partial(exchange_any, rows_dev)
        order = lambda own_row, k: k
    shape = jax.ShapeDtypeStruct
    cur_shape, part_shape = shape((rows_dev, n, n), F32), shape((n, n), F32)
    greater = greater_rows.reshape(steps * rows_dev * n, n)
    shape, vmem, hbm = jax.ShapeDtypeStruct, pltpu.VMEM, pltpu.HBM
    cur = (shape((rows_dev, n, n), F32), vmem)
    part_out = (shape((n, n), F32), vmem)
    parts = [vmem((n, 2 * rows_dev * n), BF16)] * 2
    current, wide, active, strength, ham, part = call(
        functools.partial(first_kernel, rows_dev, n, steps),
        [hbm] * 8,
        [cur, (shape((2 * rows_dev * n, 2 * n), BF16), vmem), (shape((steps * rows_dev, n), F32), vmem),
         (shape((n, n), F32), vmem), (shape((n, 2 * n), BF16), vmem), part_out],
        parts + [pltpu.SMEM((1,), jnp.int32)] * 2 + [vmem((n, n), F32)] * 2 + [vmem(flat, F32)] * 2
        + [vmem((2 * rows_dev * n, n), F32), pltpu.SemaphoreType.DMA((4 + 4 * PARTS,))],
        "first_step",
    )(*[x if x.ndim == 1 else pltpu.with_memory_space_constraint(x, hbm) for x in (
        step_index, cutoff, lesser.reshape(flat), advanced.reshape(flat), first_row.reshape(flat), greater, coupling, hamiltonian
    )])
    for section in range(1, steps):
        pieces = exchange(part)
        current, part = call(
            functools.partial(next_kernel, section, rows_dev, n, order),
            [vmem] * (6 + rows_dev), [cur, part_out], parts, "next_step",
        )(current, greater, active, strength, ham, wide, *pieces)
    pieces = exchange(part)
    final = call(
        functools.partial(last_kernel, rows_dev, n, order),
        [vmem] * (1 + rows_dev), [(shape(flat, F32), hbm)], [vmem(flat, F32), pltpu.SemaphoreType.DMA((PARTS,))], "last_step",
    )(current, *pieces)[0]
    return final.reshape(first_row.shape)


def solution(mesh):
    in_specs = (
        P("col", None, "hist", None),
        P("col", None, "hist", None),
        P(None, "col", None),
        P(None, None, "col", None),
        P(),
        P(),
        P("hist"),
        P(),
    )
    return jax.shard_map(
        functools.partial(on_device, mesh.shape["hist"], mesh.shape["col"]),
        mesh=mesh, in_specs=in_specs, out_specs=P(None, "col", None), check_vma=False,
    )
```

```python
import functools

import jax
import jax.numpy as jnp
from jax import lax
from jax.experimental import pallas as pl
from jax.experimental.pallas import tpu as pltpu
from jax.sharding import PartitionSpec as P

STEP_SIZE = 0.2
BF16 = jnp.bfloat16
F32 = jnp.float32
VMEM_BYTES = 12 * 2**20
PARTS = 4


def split(x):
    high = x.astype(BF16)
    return high, (x - high.astype(F32)).astype(BF16)


def times_wide(high, low, wide):
    n = wide.shape[-1] // 2
    first = jnp.dot(high, wide, preferred_element_type=F32)
    second = jnp.dot(low, wide[:, :n], preferred_element_type=F32)
    return first[:, :n] + first[:, n:] + second


def advance(section, rows_dev, n, owner, own_row, cur, g_ref, active_ref, strength_ref, ham_ref, wide_ref, part_ref, high_ref, low_ref):
    strength = strength_ref[...]
    for s in range(rows_dev):
        x = cur[s]
        g = g_ref[pl.ds(s, n, stride=rows_dev), :]
        active = active_ref[pl.ds(section * rows_dev + s, 1), :]
        u = strength * x * g
        less = -(u * x)
        ret = (u * x - u * g) * active
        for where, value in ((s, ret), (rows_dev + s, less)):
            high, low = split(value)
            high_ref[:, where * n : (where + 1) * n] = high
            low_ref[:, where * n : (where + 1) * n] = low
    total = times_wide(high_ref[...], low_ref[...], wide_ref[...])
    row = cur[own_row] * owner
    row_wide = jnp.concatenate(split(row), axis=1)
    part_ref[...] = total + times_wide(ham_ref[:, :n], ham_ref[:, n:], row_wide)


def places(rows_dev):
    hist_pos, col_pos = lax.axis_index("hist"), lax.axis_index("col")
    own_row = lax.rem(hist_pos, rows_dev)
    owner = jnp.where(lax.div(hist_pos, rows_dev) == col_pos, 1.0, 0.0).astype(F32)
    return own_row, owner, col_pos


def first_kernel(rows_dev, n, steps, step_hbm, cutoff_hbm, lesser_hbm, adv_hbm, first_hbm, g_hbm, coup_hbm, ham_hbm,
                 cur_ref, wide_ref, active_ref, strength_ref, ham_ref, part_ref,
                 high_ref, low_ref, step_ref, cutoff_ref, coup_ref, h_ref, first_ref, g_ref, table_ref, sems):
    sources = [(step_hbm, step_ref), (cutoff_hbm, cutoff_ref), (coup_hbm, coup_ref), (ham_hbm, h_ref)]
    half = rows_dev * n // PARTS
    for part in range(PARTS):
        rows = pl.ds(part * half, half)
        sources += [(first_hbm.at[rows], first_ref.at[rows]), (g_hbm.at[rows], g_ref.at[rows])]
    for table, source in enumerate((lesser_hbm, adv_hbm)):
        for part in range(PARTS):
            rows = pl.ds(part * half, half)
            sources.append((source.at[rows], table_ref.at[pl.ds(table * rows_dev * n + part * half, half)]))
    copies = [pltpu.make_async_copy(a, b, sems.at[k]) for k, (a, b) in enumerate(sources)]
    for copy in copies:
        copy.start()
    own_row, owner, col_pos = places(rows_dev)
    for copy in copies[:4]:
        copy.wait()
    cutoff, start = cutoff_ref[0], step_ref[0]
    coup = coup_ref[...]
    strength_ref[...] = coup * coup
    ham_ref[...] = jnp.concatenate(split(h_ref[...]), axis=1)
    for q in range(steps):
        for s in range(rows_dev):
            active_ref[q * rows_dev + s : q * rows_dev + s + 1, :] = jnp.full(
                (1, n), jnp.where(col_pos * rows_dev + s < start + q, 1.0, 0.0).astype(F32)
            )
    for copy in copies[4 : 4 + 2 * PARTS]:
        copy.wait()
    for s in range(rows_dev):
        cur_ref[s] = first_ref[pl.ds(s, n, stride=rows_dev), :]
    for table in range(2):
        for part in range(PARTS):
            copies[4 + (2 + table) * PARTS + part].wait()
            for s in range(part * rows_dev // PARTS, (part + 1) * rows_dev // PARTS):
                inside = jnp.where(col_pos * rows_dev + s < cutoff, 1.0, 0.0).astype(F32)
                where = (table * rows_dev + s) * n
                value = table_ref[where : where + n, :]
                wide_ref[where : where + n, :] = jnp.concatenate(split(value * inside if table else value), axis=1)
    advance(0, rows_dev, n, owner, own_row, cur_ref, g_ref, active_ref, strength_ref, ham_ref, wide_ref, part_ref, high_ref, low_ref)


def next_kernel(section, rows_dev, n, order, prev_ref, greater_ref, active_ref, strength_ref, ham_ref, wide_ref, *rest):
    pieces, (cur_ref, part_ref, high_ref, low_ref) = rest[:rows_dev], rest[rows_dev:]
    own_row, owner, _ = places(rows_dev)
    for k, piece in enumerate(pieces):
        s = order(own_row, k)
        cur_ref[s] = prev_ref[s] - STEP_SIZE * piece[...]
    g_ref = greater_ref.at[pl.ds(section * rows_dev * n, rows_dev * n)]
    advance(section, rows_dev, n, owner, own_row, cur_ref, g_ref, active_ref, strength_ref, ham_ref, wide_ref, part_ref, high_ref, low_ref)


def last_kernel(rows_dev, n, order, prev_ref, *rest):
    pieces, (out_hbm, out_ref, sems) = rest[:rows_dev], rest[rows_dev:]
    own_row, _, _ = places(rows_dev)
    size = n // PARTS
    copies = []
    for part in range(PARTS):
        rows = pl.ds(part * size, size)
        for k, piece in enumerate(pieces):
            s = order(own_row, k)
            out_ref[pl.ds(part * size * rows_dev + s, size, stride=rows_dev), :] = prev_ref[s, rows, :] - STEP_SIZE * piece[rows, :]
        flat = pl.ds(part * size * rows_dev, size * rows_dev)
        copies.append(pltpu.make_async_copy(out_ref.at[flat], out_hbm.at[flat], sems.at[part]))
        copies[-1].start()
    for copy in copies:
        copy.wait()


def call(kernel, ins, outs, scratch, name):
    return pl.pallas_call(
        kernel,
        out_shape=[shape for shape, _ in outs],
        in_specs=[pl.BlockSpec(memory_space=space) for space in ins],
        out_specs=[pl.BlockSpec(memory_space=space) for _, space in outs],
        scratch_shapes=scratch,
        compiler_params=pltpu.CompilerParams(vmem_limit_bytes=VMEM_BYTES),
        name=name,
    )


def exchange_pairs(hist, rows_dev, part):
    def at(h, c):
        return h * 2 + c

    def moved(x, pairs):
        return lax.ppermute(x, ("hist", "col"), pairs)

    def flip(x, bits):
        return moved(x, [(at(h, c), at(h ^ bits, c)) for h in range(hist) for c in range(2)])

    def block(h):
        return h // rows_dev

    cycle = [(at(h, 1 - block(h)), at(h, block(h))) for h in range(hist)]
    cycle += [(at(h, block(h)), at(h ^ rows_dev, block(h))) for h in range(hist)]
    across = [(at(h, 1 - block(h)), at(h ^ rows_dev, block(h))) for h in range(hist)]
    across += [(at(h, block(h)), at(h, block(h))) for h in range(hist)]
    own = moved(part, across) + moved(part, cycle)
    pieces = [own] + [None] * (rows_dev - 1)
    for bits in range(2, rows_dev, 2):
        pieces[bits] = flip(own, bits)
    for bits in range(0, rows_dev, 2):
        pieces[bits + 1] = flip(pieces[bits], 1)
    return pieces


def exchange_any(rows_dev, part):
    total = lax.psum(part, "col")
    rows = lax.all_gather(total, "hist", axis=0)
    block = lax.dynamic_slice_in_dim(rows, lax.axis_index("col") * rows_dev, rows_dev, axis=0)
    return [block[s] for s in range(rows_dev)]


def on_device(hist, cols, lesser, advanced, first_row, greater_rows, hamiltonian, coupling, cutoff, step_index):
    rows_dev, n, cols_dev, _ = lesser.shape
    steps = greater_rows.shape[0]
    assert cols_dev == 1 and hist == cols * rows_dev
    flat = (rows_dev * n, n)
    pairs = cols == 2 and hist & (hist - 1) == 0 and rows_dev >= 2
    if pairs:
        exchange = functools.partial(exchange_pairs, hist, rows_dev)
        order = lambda own_row, k: jnp.bitwise_xor(own_row, k)
    else:
        exchange = functools.partial(exchange_any, rows_dev)
        order = lambda own_row, k: k
    shape = jax.ShapeDtypeStruct
    cur_shape, part_shape = shape((rows_dev, n, n), F32), shape((n, n), F32)
    greater = greater_rows.reshape(steps * rows_dev * n, n)
    shape, vmem, hbm = jax.ShapeDtypeStruct, pltpu.VMEM, pltpu.HBM
    cur = (shape((rows_dev, n, n), F32), vmem)
    part_out = (shape((n, n), F32), vmem)
    parts = [vmem((n, 2 * rows_dev * n), BF16)] * 2
    current, wide, active, strength, ham, part = call(
        functools.partial(first_kernel, rows_dev, n, steps),
        [hbm] * 8,
        [cur, (shape((2 * rows_dev * n, 2 * n), BF16), vmem), (shape((steps * rows_dev, n), F32), vmem),
         (shape((n, n), F32), vmem), (shape((n, 2 * n), BF16), vmem), part_out],
        parts + [pltpu.SMEM((1,), jnp.int32)] * 2 + [vmem((n, n), F32)] * 2 + [vmem(flat, F32)] * 2
        + [vmem((2 * rows_dev * n, n), F32), pltpu.SemaphoreType.DMA((4 + 4 * PARTS,))],
        "first_step",
    )(*[x if x.ndim == 1 else pltpu.with_memory_space_constraint(x, hbm) for x in (
        step_index, cutoff, lesser.reshape(flat), advanced.reshape(flat), first_row.reshape(flat), greater, coupling, hamiltonian
    )])
    for section in range(1, steps):
        pieces = exchange(part)
        current, part = call(
            functools.partial(next_kernel, section, rows_dev, n, order),
            [vmem] * (6 + rows_dev), [cur, part_out], parts, "next_step",
        )(current, greater, active, strength, ham, wide, *pieces)
    pieces = exchange(part)
    final = call(
        functools.partial(last_kernel, rows_dev, n, order),
        [vmem] * (1 + rows_dev), [(shape(flat, F32), hbm)], [vmem(flat, F32), pltpu.SemaphoreType.DMA((PARTS,))], "last_step",
    )(current, *pieces)[0]
    return final.reshape(first_row.shape)


def solution(mesh):
    in_specs = (
        P("col", None, "hist", None),
        P("col", None, "hist", None),
        P(None, "col", None),
        P(None, None, "col", None),
        P(),
        P(),
        P("hist"),
        P(),
    )
    return jax.shard_map(
        functools.partial(on_device, mesh.shape["hist"], mesh.shape["col"]),
        mesh=mesh, in_specs=in_specs, out_specs=P(None, "col", None), check_vma=False,
    )
```

```python
import functools

import jax
import jax.numpy as jnp
from jax import lax
from jax.experimental import pallas as pl
from jax.experimental.pallas import tpu as pltpu
from jax.sharding import PartitionSpec as P

STEP_SIZE = 0.2
PRECISE = lax.Precision.HIGHEST
BF16 = jnp.bfloat16
F32 = jnp.float32
VMEM_BYTES = 12 * 2**20


def split(x):
    high = x.astype(BF16)
    return high, (x - high.astype(F32)).astype(BF16)


def tall(x):
    return jnp.concatenate(split(x), axis=0)


def wide(x):
    return jnp.concatenate(split(x), axis=1)


def product(rows, columns):
    m, n = rows.shape[0] // 2, columns.shape[1] // 2
    both = jnp.dot(rows, columns, preferred_element_type=F32)
    return both[:m, :n] + (both[:m, n:] + both[m:, :n])


def places(rows_dev):
    hist_pos = lax.axis_index("hist")
    return lax.rem(hist_pos, rows_dev), lax.rem(hist_pos, 2), lax.axis_index("col")


def every(first, s, half, rows_dev):
    return pl.ds(first * rows_dev + s, half, stride=rows_dev)


def sigmas(section, rows_dev, half, core, cur, g_ref, g_first, active_ref, strength_ref, sigma_ref):
    n = 2 * half
    strength = strength_ref[...]
    for s in range(rows_dev):
        x = cur[s]
        g = g_ref[every(g_first + core * half, s, half, rows_dev), :]
        u = strength * x * g
        less = -(u * x)
        ret = (u * x - u * g) * active_ref[pl.ds(section * rows_dev + s, 1), :]
        for where, value in ((s, ret), (rows_dev + s, less)):
            sigma_ref[:, where * n : (where + 1) * n] = tall(value)


def split_tables(rows_dev, n, col_pos, cutoff, lesser_ref, adv_ref, wide_ref):
    for s in range(rows_dev):
        inside = jnp.where(col_pos * rows_dev + s < cutoff, 1.0, 0.0).astype(F32)
        wide_ref[s * n : (s + 1) * n, :] = wide(lesser_ref[s * n : (s + 1) * n, :])
        wide_ref[(rows_dev + s) * n : (rows_dev + s + 1) * n, :] = wide(adv_ref[s * n : (s + 1) * n, :] * inside)


def first_kernel(rows_dev, half, steps, limits_ref, lesser_hbm, adv_hbm, first_hbm, greater_hbm, coup_hbm, ham_hbm,
                 cur_ref, wide_ref, active_ref, strength_ref, ham_ref, turned_ref, sigma_ref, own_ref,
                 lesser_ref, adv_ref, first_ref, g_ref, h_ref, sems):
    n = 2 * half
    own_row, core, col_pos = places(rows_dev)
    mine, other = core * half, (1 - core) * half
    rows = pl.ds(pl.multiple_of(mine, half), half)
    copies = [
        pltpu.make_async_copy(source, target, sems.at[k])
        for k, (source, target) in enumerate((
            (coup_hbm.at[rows], strength_ref),
            (ham_hbm.at[rows], h_ref),
            (first_hbm, first_ref),
            (greater_hbm.at[pl.ds(0, rows_dev * n)], g_ref),
            (lesser_hbm, lesser_ref),
            (adv_hbm, adv_ref),
        ))
    ]
    for copy in copies:
        copy.start()
    start, cutoff = limits_ref[0:1, :], limits_ref[1:2, :]
    for q in range(steps):
        for s in range(rows_dev):
            active_ref[q * rows_dev + s : q * rows_dev + s + 1, :] = jnp.where(
                col_pos * rows_dev + s < start + q, 1.0, 0.0
            ).astype(F32)
    for copy in copies[:4]:
        copy.wait()
    strength_ref[...] = strength_ref[...] * strength_ref[...]
    ham = h_ref[...]
    ham = tall(jnp.where(core == 0, ham, pltpu.roll(ham, half, 1)))
    ham_ref[...] = ham
    for s in range(rows_dev):
        cur_ref[s] = first_ref[every(mine, s, half, rows_dev), :]
    sigmas(0, rows_dev, half, core, cur_ref, g_ref, 0, active_ref, strength_ref, sigma_ref)
    for j in range(2):
        s = jnp.bitwise_xor(own_row, j)
        whole = jnp.concatenate(
            [first_ref[every(mine, s, half, rows_dev), :], first_ref[every(other, s, half, rows_dev), :]], axis=0
        )
        turned_ref[j * half : (j + 1) * half, :] = product(ham, wide(whole))
    for copy in copies[4:]:
        copy.wait()
    split_tables(rows_dev, n, col_pos, cutoff, lesser_ref, adv_ref, wide_ref)
    own_ref[...] = product(sigma_ref[...], wide_ref[...])


def second_kernel(rows_dev, half, limits_ref, lesser_ref, adv_ref, sigma_ref, own_ref, wide_ref, part_ref):
    col_pos = lax.axis_index("col")
    split_tables(rows_dev, 2 * half, col_pos, limits_ref[1:2, :], lesser_ref, adv_ref, wide_ref)
    part_ref[:half, :] = own_ref[...]
    part_ref[half:, :] = product(sigma_ref[...], wide_ref[...])


def next_kernel(section, rows_dev, half, prev_ref, greater_ref, active_ref, strength_ref, own_wide_ref, other_wide_ref, *rest):
    pieces, (cur_ref, mine_ref, part_ref, sigma_ref) = rest[: rows_dev // 2], rest[rows_dev // 2 :]
    own_row, core, _ = places(rows_dev)
    for k, piece in enumerate(pieces):
        for j in range(2):
            s = jnp.bitwise_xor(own_row, 2 * k + j)
            new = prev_ref[s] - STEP_SIZE * piece[j * half : (j + 1) * half, :]
            cur_ref[s] = new
            if k == 0:
                mine_ref[j * half : (j + 1) * half, :] = new
    sigmas(section, rows_dev, half, core, cur_ref, greater_ref, section * 2 * half, active_ref, strength_ref, sigma_ref)
    part_ref[:half, :] = product(sigma_ref[...], own_wide_ref[...])
    part_ref[half:, :] = product(sigma_ref[...], other_wide_ref[...])


def turn_kernel(half, ham_ref, mine_ref, other_ref, turned_ref):
    ham = ham_ref[...]
    for j in range(2):
        whole = jnp.concatenate(
            [mine_ref[j * half : (j + 1) * half, :], other_ref[(1 - j) * half : (2 - j) * half, :]], axis=0
        )
        turned_ref[j * half : (j + 1) * half, :] = product(ham, wide(whole))


def last_kernel(rows_dev, half, *refs):
    count = rows_dev // 2
    own_row, core, _ = places(rows_dev)
    out_hbm, out_ref, sems = refs[-3:]
    copies = []
    for away in range(2):
        prev_ref, pieces = refs[away], refs[2 + away * count : 2 + (away + 1) * count]
        side = jnp.bitwise_xor(core, away) * half
        for k, piece in enumerate(pieces):
            for j in range(2):
                s = jnp.bitwise_xor(own_row, (2 * k + j) ^ away)
                new = prev_ref[s] - STEP_SIZE * piece[j * half : (j + 1) * half, :]
                out_ref[every(side, s, half, rows_dev), :] = new
        flat = pl.ds(pl.multiple_of(side * rows_dev, half * rows_dev), half * rows_dev)
        copies.append(pltpu.make_async_copy(out_ref.at[flat], out_hbm.at[flat], sems.at[away]))
        copies[-1].start()
    for copy in copies:
        copy.wait()


def call(kernel, ins, outs, scratch, name):
    return pl.pallas_call(
        kernel,
        out_shape=[shape for shape, _ in outs],
        in_specs=[pl.BlockSpec(memory_space=space) for space in ins],
        out_specs=[pl.BlockSpec(memory_space=space) for _, space in outs],
        scratch_shapes=scratch,
        compiler_params=pltpu.CompilerParams(vmem_limit_bytes=VMEM_BYTES),
        name=name,
    )


def in_pairs(hist, lesser, advanced, first_row, greater_rows, hamiltonian, coupling, cutoff, step_index):
    rows_dev, n = lesser.shape[:2]
    steps, half = greater_rows.shape[0], n // 2
    flat = (rows_dev * n, n)
    shape, vmem, hbm = jax.ShapeDtypeStruct, pltpu.VMEM, pltpu.HBM

    def at(h, c):
        return h * 2 + c

    def block(h):
        return h // rows_dev

    def moved(x, pairs):
        return lax.ppermute(x, ("hist", "col"), pairs)

    def flip(x, bits):
        return moved(x, [(at(h, c), at(h ^ bits, c)) for h in range(hist) for c in range(2)])

    cycle = [(at(h, 1 - block(h)), at(h, block(h))) for h in range(hist)]
    cycle += [(at(h, block(h)), at(h ^ rows_dev, block(h))) for h in range(hist)]
    across = [(at(h, 1 - block(h)), at(h ^ rows_dev, block(h))) for h in range(hist)]
    across += [(at(h, block(h)), at(h, block(h))) for h in range(hist)]

    def exchange(part, turned):
        own = moved(part, across) + moved(part, cycle) + turned
        return [own] + [flip(own, bits) for bits in range(2, rows_dev, 2)]

    def out(dims, kind=F32):
        return shape(dims, kind), vmem

    greater = greater_rows.reshape(steps * rows_dev * n, n)
    tables = lesser.reshape(flat), advanced.reshape(flat)
    limits = jnp.broadcast_to(jnp.concatenate([step_index, cutoff])[:, None], (2, n))
    cur_out, pair_out, wide_out = out((rows_dev, half, n)), out((n, n)), out((2 * rows_dev * n, 2 * n), BF16)
    sigma = (n, 2 * rows_dev * n)
    current, own_wide, active, strength, ham, turned, first_sigma, own_part = call(
        functools.partial(first_kernel, rows_dev, half, steps),
        [vmem] + [hbm] * 6,
        [cur_out, wide_out, out((steps * rows_dev, n)), out((half, n)), out((n, n), BF16), pair_out, out(sigma, BF16), out((half, n))],
        [vmem(flat, F32)] * 4 + [vmem((half, n), F32), pltpu.SemaphoreType.DMA((6,))],
        "first_step",
    )(limits, *[
        pltpu.with_memory_space_constraint(x, hbm)
        for x in (*tables, first_row.reshape(flat), greater, coupling, hamiltonian)
    ])
    other_wide, part = call(
        functools.partial(second_kernel, rows_dev, half),
        [vmem] * 5, [wide_out, pair_out], [], "first_step_other",
    )(flip(limits, 1), *[flip(x, 1) for x in tables], first_sigma, own_part)
    for section in range(1, steps):
        pieces = exchange(part, turned)
        current, mine, part = call(
            functools.partial(next_kernel, section, rows_dev, half),
            [vmem] * (6 + rows_dev // 2), [cur_out, pair_out, pair_out], [vmem(sigma, BF16)], "next_step",
        )(current, greater, active, strength, own_wide, other_wide, *pieces)
        turned = call(functools.partial(turn_kernel, half), [vmem] * 3, [pair_out], [], "turn")(ham, mine, flip(mine, 1))[0]
    pieces = exchange(part, turned)
    final = call(
        functools.partial(last_kernel, rows_dev, half),
        [vmem] * (2 + rows_dev), [(shape(flat, F32), hbm)], [vmem(flat, F32), pltpu.SemaphoreType.DMA((2,))], "last_step",
    )(current, flip(current, 1), *pieces, *[flip(x, 1) for x in pieces])[0]
    return final.reshape(first_row.shape)


def in_general(lesser, advanced, first_row, greater_rows, hamiltonian, coupling, cutoff, step_index):
    rows_dev, orbitals, cols_dev, _ = lesser.shape
    row_times = lax.axis_index("col") * rows_dev + jnp.arange(rows_dev, dtype=jnp.int32)
    inside = (row_times[:, None] < cutoff[None, :]).astype(F32)
    adv_flat = (advanced * inside[:, None, :, None]).reshape(rows_dev * orbitals, cols_dev * orbitals)
    hist_flat = lesser.reshape(rows_dev * orbitals, cols_dev * orbitals)
    propagator = jnp.eye(orbitals, dtype=F32) - STEP_SIZE * hamiltonian
    strength = (coupling * coupling)[:, None, :]
    current = first_row
    for section in range(greater_rows.shape[0]):
        greater = greater_rows[section]
        sigma_less = -strength * current * current * greater
        sigma_ret = -strength * greater * greater * current - sigma_less
        active = (row_times < step_index[0] + section).astype(F32)
        ret_flat = (sigma_ret * active[None, :, None]).reshape(orbitals, rows_dev * orbitals)
        less_flat = sigma_less.reshape(orbitals, rows_dev * orbitals)
        memory = jnp.dot(ret_flat, hist_flat, precision=PRECISE, preferred_element_type=F32)
        memory = memory + jnp.dot(less_flat, adv_flat, precision=PRECISE, preferred_element_type=F32)
        share = lax.psum_scatter(memory.reshape(orbitals, cols_dev, orbitals), "col", scatter_dimension=0, tiled=True)
        spread = lax.all_gather(share, "hist", axis=1, tiled=True)
        memory_block = lax.all_to_all(spread, "col", split_axis=1, concat_axis=0, tiled=True)
        moved = jnp.einsum("ik,ksj->isj", propagator, current, precision=PRECISE)
        current = moved - STEP_SIZE * memory_block
    return current


def solution(mesh):
    hist, cols = mesh.shape["hist"], mesh.shape["col"]

    def on_device(lesser, *rest):
        rows_dev, _, cols_dev, _ = lesser.shape
        if cols == 2 and cols_dev == 1 and hist == 2 * rows_dev and hist & (hist - 1) == 0 and rows_dev > 1:
            return in_pairs(hist, lesser, *rest)
        return in_general(lesser, *rest)

    in_specs = (
        P("col", None, "hist", None),
        P("col", None, "hist", None),
        P(None, "col", None),
        P(None, None, "col", None),
        P(),
        P(),
        P("hist"),
        P(),
    )
    return jax.shard_map(on_device, mesh=mesh, in_specs=in_specs, out_specs=P(None, "col", None), check_vma=False)
```

```python
import functools

import jax
import jax.numpy as jnp
from jax import lax
from jax.experimental import pallas as pl
from jax.experimental.pallas import tpu as pltpu
from jax.sharding import PartitionSpec as P

STEP_SIZE = 0.2
PRECISE = lax.Precision.HIGHEST
BF16 = jnp.bfloat16
F32 = jnp.float32
VMEM_BYTES = 12 * 2**20


def split(x):
    high = x.astype(BF16)
    return high, (x - high.astype(F32)).astype(BF16)


def tall(x):
    return jnp.concatenate(split(x), axis=0)


def wide(x):
    return jnp.concatenate(split(x), axis=1)


def product(rows, columns):
    m, n = rows.shape[0] // 2, columns.shape[1] // 2
    both = jnp.dot(rows, columns, preferred_element_type=F32)
    return both[:m, :n] + (both[:m, n:] + both[m:, :n])


def places(rows_dev):
    hist_pos = lax.axis_index("hist")
    return lax.rem(hist_pos, rows_dev), lax.rem(hist_pos, 2), lax.axis_index("col")


def every(first, s, half, rows_dev):
    return pl.ds(first * rows_dev + s, half, stride=rows_dev)


def sigmas(section, rows_dev, half, core, cur, g_ref, g_first, active_ref, strength_ref, sigma_ref):
    n = 2 * half
    strength = strength_ref[...]
    for s in range(rows_dev):
        x = cur[s]
        g = g_ref[every(g_first + core * half, s, half, rows_dev), :]
        u = strength * x * g
        less = -(u * x)
        ret = (u * x - u * g) * active_ref[pl.ds(section * rows_dev + s, 1), :]
        for where, value in ((s, ret), (rows_dev + s, less)):
            sigma_ref[:, where * n : (where + 1) * n] = tall(value)


def split_tables(rows_dev, n, col_pos, cutoff, lesser_ref, adv_ref, wide_ref):
    for s in range(rows_dev):
        inside = jnp.where(col_pos * rows_dev + s < cutoff, 1.0, 0.0).astype(F32)
        wide_ref[s * n : (s + 1) * n, :] = wide(lesser_ref[s * n : (s + 1) * n, :])
        wide_ref[(rows_dev + s) * n : (rows_dev + s + 1) * n, :] = wide(adv_ref[s * n : (s + 1) * n, :] * inside)


def turn(half, ham_ref, near_ref, turned_ref):
    for j in range(2):
        turned_ref[j * half : (j + 1) * half, :] = product(ham_ref[...], wide(near_ref[j]))


def first_kernel(rows_dev, half, steps, limits_ref, lesser_hbm, adv_hbm, first_hbm, greater_hbm, coup_hbm, ham_hbm,
                 cur_ref, wide_ref, active_ref, strength_ref, ham_ref, near_ref, turned_ref, sigma_ref, own_ref,
                 lesser_ref, adv_ref, first_ref, g_ref, h_ref, sems):
    n = 2 * half
    own_row, core, col_pos = places(rows_dev)
    mine, other = core * half, (1 - core) * half
    rows = pl.ds(pl.multiple_of(mine, half), half)
    copies = [
        pltpu.make_async_copy(source, target, sems.at[k])
        for k, (source, target) in enumerate((
            (coup_hbm.at[rows], strength_ref),
            (ham_hbm.at[rows], h_ref),
            (first_hbm, first_ref),
            (greater_hbm.at[pl.ds(0, rows_dev * n)], g_ref),
            (lesser_hbm, lesser_ref),
            (adv_hbm, adv_ref),
        ))
    ]
    for copy in copies:
        copy.start()
    start, cutoff = limits_ref[0:1, :], limits_ref[1:2, :]
    for q in range(steps):
        for s in range(rows_dev):
            active_ref[q * rows_dev + s : q * rows_dev + s + 1, :] = jnp.where(
                col_pos * rows_dev + s < start + q, 1.0, 0.0
            ).astype(F32)
    for copy in copies[:4]:
        copy.wait()
    strength_ref[...] = strength_ref[...] * strength_ref[...]
    ham = h_ref[...]
    ham = tall(jnp.where(core == 0, ham, pltpu.roll(ham, half, 1)))
    ham_ref[...] = ham
    for s in range(rows_dev):
        cur_ref[s] = first_ref[every(mine, s, half, rows_dev), :]
    sigmas(0, rows_dev, half, core, cur_ref, g_ref, 0, active_ref, strength_ref, sigma_ref)
    for j in range(2):
        s = jnp.bitwise_xor(own_row, j)
        near_ref[j, :half, :] = first_ref[every(mine, s, half, rows_dev), :]
        near_ref[j, half:, :] = first_ref[every(other, s, half, rows_dev), :]
    turn(half, ham_ref, near_ref, turned_ref)
    for copy in copies[4:]:
        copy.wait()
    split_tables(rows_dev, n, col_pos, cutoff, lesser_ref, adv_ref, wide_ref)
    own_ref[...] = product(sigma_ref[...], wide_ref[...])


def second_kernel(rows_dev, half, limits_ref, lesser_ref, adv_ref, sigma_ref, own_ref, wide_ref, part_ref):
    col_pos = lax.axis_index("col")
    split_tables(rows_dev, 2 * half, col_pos, limits_ref[1:2, :], lesser_ref, adv_ref, wide_ref)
    part_ref[:half, :] = own_ref[...]
    part_ref[half:, :] = product(sigma_ref[...], wide_ref[...])


def next_kernel(section, rows_dev, half, prev_ref, prev_near_ref, greater_ref, active_ref, strength_ref, own_wide_ref, other_wide_ref, *rest):
    own_ref, swapped_ref, *others = rest[: rows_dev // 2 + 1]
    cur_ref, near_ref, part_ref, sigma_ref = rest[rows_dev // 2 + 1 :]
    own_row, core, _ = places(rows_dev)
    for k, piece in enumerate([own_ref] + others):
        for j in range(2):
            s = jnp.bitwise_xor(own_row, 2 * k + j)
            cur_ref[s] = prev_ref[s] - STEP_SIZE * piece[j * half : (j + 1) * half, :]
    for j in range(2):
        near_ref[j, :half, :] = prev_near_ref[j, :half, :] - STEP_SIZE * own_ref[j * half : (j + 1) * half, :]
        near_ref[j, half:, :] = prev_near_ref[j, half:, :] - STEP_SIZE * swapped_ref[(1 - j) * half : (2 - j) * half, :]
    sigmas(section, rows_dev, half, core, cur_ref, greater_ref, section * 2 * half, active_ref, strength_ref, sigma_ref)
    part_ref[:half, :] = product(sigma_ref[...], own_wide_ref[...])
    part_ref[half:, :] = product(sigma_ref[...], other_wide_ref[...])


def last_kernel(rows_dev, half, *refs):
    count = rows_dev // 2
    own_row, core, _ = places(rows_dev)
    out_hbm, out_ref, sems = refs[-3:]
    copies = []
    for away in range(2):
        prev_ref, pieces = refs[away], refs[2 + away * count : 2 + (away + 1) * count]
        side = jnp.bitwise_xor(core, away) * half
        for k, piece in enumerate(pieces):
            for j in range(2):
                s = jnp.bitwise_xor(own_row, (2 * k + j) ^ away)
                new = prev_ref[s] - STEP_SIZE * piece[j * half : (j + 1) * half, :]
                out_ref[every(side, s, half, rows_dev), :] = new
        flat = pl.ds(pl.multiple_of(side * rows_dev, half * rows_dev), half * rows_dev)
        copies.append(pltpu.make_async_copy(out_ref.at[flat], out_hbm.at[flat], sems.at[away]))
        copies[-1].start()
    for copy in copies:
        copy.wait()


def call(kernel, ins, outs, scratch, name):
    return pl.pallas_call(
        kernel,
        out_shape=[shape for shape, _ in outs],
        in_specs=[pl.BlockSpec(memory_space=space) for space in ins],
        out_specs=[pl.BlockSpec(memory_space=space) for _, space in outs],
        scratch_shapes=scratch,
        compiler_params=pltpu.CompilerParams(vmem_limit_bytes=VMEM_BYTES),
        name=name,
    )


def in_pairs(hist, lesser, advanced, first_row, greater_rows, hamiltonian, coupling, cutoff, step_index):
    rows_dev, n = lesser.shape[:2]
    steps, half = greater_rows.shape[0], n // 2
    flat = (rows_dev * n, n)
    shape, vmem, hbm = jax.ShapeDtypeStruct, pltpu.VMEM, pltpu.HBM

    def at(h, c):
        return h * 2 + c

    def block(h):
        return h // rows_dev

    def moved(x, pairs):
        return lax.ppermute(x, ("hist", "col"), pairs)

    def flip(x, bits):
        return moved(x, [(at(h, c), at(h ^ bits, c)) for h in range(hist) for c in range(2)])

    cycle = [(at(h, 1 - block(h)), at(h, block(h))) for h in range(hist)]
    cycle += [(at(h, block(h)), at(h ^ rows_dev, block(h))) for h in range(hist)]
    across = [(at(h, 1 - block(h)), at(h ^ rows_dev, block(h))) for h in range(hist)]
    across += [(at(h, block(h)), at(h, block(h))) for h in range(hist)]

    def exchange(part, turned):
        own = moved(part, across) + moved(part, cycle) + turned
        return [own, flip(own, 1)] + [flip(own, bits) for bits in range(2, rows_dev, 2)]

    def out(dims, kind=F32):
        return shape(dims, kind), vmem

    greater = greater_rows.reshape(steps * rows_dev * n, n)
    tables = lesser.reshape(flat), advanced.reshape(flat)
    limits = jnp.broadcast_to(jnp.concatenate([step_index, cutoff])[:, None], (2, n))
    near_out = out((2, n, n))
    cur_out, pair_out, wide_out = out((rows_dev, half, n)), out((n, n)), out((2 * rows_dev * n, 2 * n), BF16)
    sigma = (n, 2 * rows_dev * n)
    current, own_wide, active, strength, ham, near, turned, first_sigma, own_part = call(
        functools.partial(first_kernel, rows_dev, half, steps),
        [vmem] + [hbm] * 6,
        [cur_out, wide_out, out((steps * rows_dev, n)), out((half, n)), out((n, n), BF16), near_out, pair_out, out(sigma, BF16), out((half, n))],
        [vmem(flat, F32)] * 4 + [vmem((half, n), F32), pltpu.SemaphoreType.DMA((6,))],
        "first_step",
    )(limits, *[
        pltpu.with_memory_space_constraint(x, hbm)
        for x in (*tables, first_row.reshape(flat), greater, coupling, hamiltonian)
    ])
    other_wide, part = call(
        functools.partial(second_kernel, rows_dev, half),
        [vmem] * 5, [wide_out, pair_out], [], "first_step_other",
    )(flip(limits, 1), *[flip(x, 1) for x in tables], first_sigma, own_part)
    for section in range(1, steps):
        pieces = exchange(part, turned)
        current, near, part = call(
            functools.partial(next_kernel, section, rows_dev, half),
            [vmem] * (8 + rows_dev // 2), [cur_out, near_out, pair_out], [vmem(sigma, BF16)], "next_step",
        )(current, near, greater, active, strength, own_wide, other_wide, *pieces)
        turned = call(functools.partial(turn, half), [vmem] * 2, [pair_out], [], "turn")(ham, near)[0]
    pieces = exchange(part, turned)
    own, swapped = [pieces[0]] + pieces[2:], pieces[1]
    final = call(
        functools.partial(last_kernel, rows_dev, half),
        [vmem] * (2 + rows_dev), [(shape(flat, F32), hbm)], [vmem(flat, F32), pltpu.SemaphoreType.DMA((2,))], "last_step",
    )(current, flip(current, 1), *own, swapped, *[flip(x, 1) for x in own[1:]])[0]
    return final.reshape(first_row.shape)


def in_general(lesser, advanced, first_row, greater_rows, hamiltonian, coupling, cutoff, step_index):
    rows_dev, orbitals, cols_dev, _ = lesser.shape
    row_times = lax.axis_index("col") * rows_dev + jnp.arange(rows_dev, dtype=jnp.int32)
    inside = (row_times[:, None] < cutoff[None, :]).astype(F32)
    adv_flat = (advanced * inside[:, None, :, None]).reshape(rows_dev * orbitals, cols_dev * orbitals)
    hist_flat = lesser.reshape(rows_dev * orbitals, cols_dev * orbitals)
    propagator = jnp.eye(orbitals, dtype=F32) - STEP_SIZE * hamiltonian
    strength = (coupling * coupling)[:, None, :]
    current = first_row
    for section in range(greater_rows.shape[0]):
        greater = greater_rows[section]
        sigma_less = -strength * current * current * greater
        sigma_ret = -strength * greater * greater * current - sigma_less
        active = (row_times < step_index[0] + section).astype(F32)
        ret_flat = (sigma_ret * active[None, :, None]).reshape(orbitals, rows_dev * orbitals)
        less_flat = sigma_less.reshape(orbitals, rows_dev * orbitals)
        memory = jnp.dot(ret_flat, hist_flat, precision=PRECISE, preferred_element_type=F32)
        memory = memory + jnp.dot(less_flat, adv_flat, precision=PRECISE, preferred_element_type=F32)
        share = lax.psum_scatter(memory.reshape(orbitals, cols_dev, orbitals), "col", scatter_dimension=0, tiled=True)
        spread = lax.all_gather(share, "hist", axis=1, tiled=True)
        memory_block = lax.all_to_all(spread, "col", split_axis=1, concat_axis=0, tiled=True)
        moved = jnp.einsum("ik,ksj->isj", propagator, current, precision=PRECISE)
        current = moved - STEP_SIZE * memory_block
    return current


def solution(mesh):
    hist, cols = mesh.shape["hist"], mesh.shape["col"]

    def on_device(lesser, *rest):
        rows_dev, _, cols_dev, _ = lesser.shape
        if cols == 2 and cols_dev == 1 and hist == 2 * rows_dev and hist & (hist - 1) == 0 and rows_dev > 1:
            return in_pairs(hist, lesser, *rest)
        return in_general(lesser, *rest)

    in_specs = (
        P("col", None, "hist", None),
        P("col", None, "hist", None),
        P(None, "col", None),
        P(None, None, "col", None),
        P(),
        P(),
        P("hist"),
        P(),
    )
    return jax.shard_map(on_device, mesh=mesh, in_specs=in_specs, out_specs=P(None, "col", None), check_vma=False)
```

```python
import functools

import jax
import jax.numpy as jnp
from jax import lax
from jax.experimental import pallas as pl
from jax.experimental.pallas import tpu as pltpu
from jax.sharding import PartitionSpec as P

STEP_SIZE = 0.2
PRECISE = lax.Precision.HIGHEST
BF16 = jnp.bfloat16
F32 = jnp.float32
VMEM_BYTES = 12 * 2**20


def split(x):
    high = x.astype(BF16)
    return high, (x - high.astype(F32)).astype(BF16)


def tall(x):
    return jnp.concatenate(split(x), axis=0)


def wide(x):
    return jnp.concatenate(split(x), axis=1)


def product(rows, columns):
    m, n = rows.shape[0] // 2, columns.shape[1] // 2
    both = jnp.dot(rows, columns, preferred_element_type=F32)
    return both[:m, :n] + (both[:m, n:] + both[m:, :n])


def places(rows_dev):
    hist_pos = lax.axis_index("hist")
    return lax.rem(hist_pos, rows_dev), lax.rem(hist_pos, 2), lax.axis_index("col")


def every(first, s, half, rows_dev):
    return pl.ds(first * rows_dev + s, half, stride=rows_dev)


def sigmas(section, rows_dev, half, core, cur, g_ref, g_first, active_ref, strength_ref, sigma_ref):
    n = 2 * half
    strength = strength_ref[...]
    for s in range(rows_dev):
        x = cur[s]
        g = g_ref[every(g_first + core * half, s, half, rows_dev), :]
        u = strength * x * g
        less = -(u * x)
        ret = (u * x - u * g) * active_ref[pl.ds(section * rows_dev + s, 1), :]
        for where, value in ((s, ret), (rows_dev + s, less)):
            sigma_ref[:, where * n : (where + 1) * n] = tall(value)


def split_tables(rows_dev, n, col_pos, cutoff, lesser_ref, adv_ref, wide_ref):
    for s in range(rows_dev):
        inside = jnp.where(col_pos * rows_dev + s < cutoff, 1.0, 0.0).astype(F32)
        wide_ref[s * n : (s + 1) * n, :] = wide(lesser_ref[s * n : (s + 1) * n, :])
        wide_ref[(rows_dev + s) * n : (rows_dev + s + 1) * n, :] = wide(adv_ref[s * n : (s + 1) * n, :] * inside)


def turn(half, ham_ref, near_ref, part_ref, far_ref, turned_ref):
    for j in range(2):
        rows = slice(j * half, (j + 1) * half)
        turned_ref[rows, :] = product(ham_ref[...], wide(near_ref[j])) + (part_ref[rows, :] - far_ref[rows, :])


def store(rows_dev, half, parts, part_ref, far_ref):
    reads_own = lax.div(lax.axis_index("hist"), rows_dev) == lax.axis_index("col")
    for j, part in enumerate(parts):
        part_ref[j * half : (j + 1) * half, :] = part
        far_ref[j * half : (j + 1) * half, :] = jnp.where(reads_own, 0.0, part)


def first_kernel(rows_dev, half, steps, limits_ref, lesser_hbm, adv_hbm, first_hbm, greater_hbm, coup_hbm, ham_hbm,
                 cur_ref, wide_ref, active_ref, strength_ref, ham_ref, near_ref, sigma_ref, own_ref,
                 lesser_ref, adv_ref, first_ref, g_ref, h_ref, sems):
    n = 2 * half
    own_row, core, col_pos = places(rows_dev)
    mine, other = core * half, (1 - core) * half
    rows = pl.ds(pl.multiple_of(mine, half), half)
    copies = [
        pltpu.make_async_copy(source, target, sems.at[k])
        for k, (source, target) in enumerate((
            (coup_hbm.at[rows], strength_ref),
            (ham_hbm.at[rows], h_ref),
            (first_hbm, first_ref),
            (greater_hbm.at[pl.ds(0, rows_dev * n)], g_ref),
            (lesser_hbm, lesser_ref),
            (adv_hbm, adv_ref),
        ))
    ]
    for copy in copies:
        copy.start()
    start, cutoff = limits_ref[0:1, :], limits_ref[1:2, :]
    for q in range(steps):
        for s in range(rows_dev):
            active_ref[q * rows_dev + s : q * rows_dev + s + 1, :] = jnp.where(
                col_pos * rows_dev + s < start + q, 1.0, 0.0
            ).astype(F32)
    for copy in copies[:4]:
        copy.wait()
    strength_ref[...] = strength_ref[...] * strength_ref[...]
    ham = h_ref[...]
    ham = tall(jnp.where(core == 0, ham, pltpu.roll(ham, half, 1)))
    ham_ref[...] = ham
    for s in range(rows_dev):
        cur_ref[s] = first_ref[every(mine, s, half, rows_dev), :]
    sigmas(0, rows_dev, half, core, cur_ref, g_ref, 0, active_ref, strength_ref, sigma_ref)
    for j in range(2):
        s = jnp.bitwise_xor(own_row, j)
        near_ref[j, :half, :] = first_ref[every(mine, s, half, rows_dev), :]
        near_ref[j, half:, :] = first_ref[every(other, s, half, rows_dev), :]
    for copy in copies[4:]:
        copy.wait()
    split_tables(rows_dev, n, col_pos, cutoff, lesser_ref, adv_ref, wide_ref)
    own_ref[...] = product(sigma_ref[...], wide_ref[...])


def second_kernel(rows_dev, half, limits_ref, lesser_ref, adv_ref, sigma_ref, own_ref, wide_ref, part_ref, far_ref):
    col_pos = lax.axis_index("col")
    split_tables(rows_dev, 2 * half, col_pos, limits_ref[1:2, :], lesser_ref, adv_ref, wide_ref)
    store(rows_dev, half, (own_ref[...], product(sigma_ref[...], wide_ref[...])), part_ref, far_ref)


def next_kernel(section, rows_dev, half, prev_ref, prev_near_ref, greater_ref, active_ref, strength_ref, own_wide_ref, other_wide_ref, *rest):
    own_ref, swapped_ref, *others = rest[: rows_dev // 2 + 1]
    cur_ref, near_ref, part_ref, far_ref, sigma_ref = rest[rows_dev // 2 + 1 :]
    own_row, core, _ = places(rows_dev)
    for k, piece in enumerate([own_ref] + others):
        for j in range(2):
            s = jnp.bitwise_xor(own_row, 2 * k + j)
            cur_ref[s] = prev_ref[s] - STEP_SIZE * piece[j * half : (j + 1) * half, :]
    for j in range(2):
        near_ref[j, :half, :] = prev_near_ref[j, :half, :] - STEP_SIZE * own_ref[j * half : (j + 1) * half, :]
        near_ref[j, half:, :] = prev_near_ref[j, half:, :] - STEP_SIZE * swapped_ref[(1 - j) * half : (2 - j) * half, :]
    sigmas(section, rows_dev, half, core, cur_ref, greater_ref, section * 2 * half, active_ref, strength_ref, sigma_ref)
    parts = [product(sigma_ref[...], table[...]) for table in (own_wide_ref, other_wide_ref)]
    store(rows_dev, half, parts, part_ref, far_ref)


def last_kernel(rows_dev, half, *refs):
    count = rows_dev // 2
    own_row, core, _ = places(rows_dev)
    out_hbm, out_ref, sems = refs[-3:]
    copies = []
    for away in range(2):
        prev_ref, pieces = refs[away], refs[2 + away * count : 2 + (away + 1) * count]
        side = jnp.bitwise_xor(core, away) * half
        for k, piece in enumerate(pieces):
            for j in range(2):
                s = jnp.bitwise_xor(own_row, (2 * k + j) ^ away)
                new = prev_ref[s] - STEP_SIZE * piece[j * half : (j + 1) * half, :]
                out_ref[every(side, s, half, rows_dev), :] = new
        flat = pl.ds(pl.multiple_of(side * rows_dev, half * rows_dev), half * rows_dev)
        copies.append(pltpu.make_async_copy(out_ref.at[flat], out_hbm.at[flat], sems.at[away]))
        copies[-1].start()
    for copy in copies:
        copy.wait()


def call(kernel, ins, outs, scratch, name):
    return pl.pallas_call(
        kernel,
        out_shape=[shape for shape, _ in outs],
        in_specs=[pl.BlockSpec(memory_space=space) for space in ins],
        out_specs=[pl.BlockSpec(memory_space=space) for _, space in outs],
        scratch_shapes=scratch,
        compiler_params=pltpu.CompilerParams(vmem_limit_bytes=VMEM_BYTES),
        name=name,
    )


def in_pairs(hist, lesser, advanced, first_row, greater_rows, hamiltonian, coupling, cutoff, step_index):
    rows_dev, n = lesser.shape[:2]
    steps, half = greater_rows.shape[0], n // 2
    flat = (rows_dev * n, n)
    shape, vmem, hbm = jax.ShapeDtypeStruct, pltpu.VMEM, pltpu.HBM

    def at(h, c):
        return h * 2 + c

    def block(h):
        return h // rows_dev

    def moved(x, pairs):
        return lax.ppermute(x, ("hist", "col"), pairs)

    def flip(x, bits):
        return moved(x, [(at(h, c), at(h ^ bits, c)) for h in range(hist) for c in range(2)])

    cycle = [(at(h, 1 - block(h)), at(h, block(h))) for h in range(hist)]
    cycle += [(at(h, block(h)), at(h ^ rows_dev, block(h))) for h in range(hist)]
    across = [(at(h, 1 - block(h)), at(h ^ rows_dev, block(h))) for h in range(hist)]
    across += [(at(h, block(h)), at(h ^ 1, block(h))) for h in range(hist)]

    def exchange(part, far, turned):
        own = moved(part, cycle) + moved(far, across) + turned
        return [own, flip(own, 1)] + [flip(own, bits) for bits in range(2, rows_dev, 2)]

    def out(dims, kind=F32):
        return shape(dims, kind), vmem

    greater = greater_rows.reshape(steps * rows_dev * n, n)
    tables = lesser.reshape(flat), advanced.reshape(flat)
    limits = jnp.broadcast_to(jnp.concatenate([step_index, cutoff])[:, None], (2, n))
    near_out = out((2, n, n))
    cur_out, pair_out, wide_out = out((rows_dev, half, n)), out((n, n)), out((2 * rows_dev * n, 2 * n), BF16)
    sigma = (n, 2 * rows_dev * n)
    current, own_wide, active, strength, ham, near, first_sigma, own_part = call(
        functools.partial(first_kernel, rows_dev, half, steps),
        [vmem] + [hbm] * 6,
        [cur_out, wide_out, out((steps * rows_dev, n)), out((half, n)), out((n, n), BF16), near_out, out(sigma, BF16), out((half, n))],
        [vmem(flat, F32)] * 4 + [vmem((half, n), F32), pltpu.SemaphoreType.DMA((6,))],
        "first_step",
    )(limits, *[
        pltpu.with_memory_space_constraint(x, hbm)
        for x in (*tables, first_row.reshape(flat), greater, coupling, hamiltonian)
    ])
    other_wide, part, far = call(
        functools.partial(second_kernel, rows_dev, half),
        [vmem] * 5, [wide_out, pair_out, pair_out], [], "first_step_other",
    )(flip(limits, 1), *[flip(x, 1) for x in tables], first_sigma, own_part)
    def add_turned():
        return call(functools.partial(turn, half), [vmem] * 4, [pair_out], [], "turn")(ham, near, part, far)[0]

    for section in range(1, steps):
        pieces = exchange(part, far, add_turned())
        current, near, part, far = call(
            functools.partial(next_kernel, section, rows_dev, half),
            [vmem] * (8 + rows_dev // 2), [cur_out, near_out, pair_out, pair_out], [vmem(sigma, BF16)], "next_step",
        )(current, near, greater, active, strength, own_wide, other_wide, *pieces)
    pieces = exchange(part, far, add_turned())
    own, swapped = [pieces[0]] + pieces[2:], pieces[1]
    final = call(
        functools.partial(last_kernel, rows_dev, half),
        [vmem] * (2 + rows_dev), [(shape(flat, F32), hbm)], [vmem(flat, F32), pltpu.SemaphoreType.DMA((2,))], "last_step",
    )(current, flip(current, 1), *own, swapped, *[flip(x, 1) for x in own[1:]])[0]
    return final.reshape(first_row.shape)


def in_general(lesser, advanced, first_row, greater_rows, hamiltonian, coupling, cutoff, step_index):
    rows_dev, orbitals, cols_dev, _ = lesser.shape
    row_times = lax.axis_index("col") * rows_dev + jnp.arange(rows_dev, dtype=jnp.int32)
    inside = (row_times[:, None] < cutoff[None, :]).astype(F32)
    adv_flat = (advanced * inside[:, None, :, None]).reshape(rows_dev * orbitals, cols_dev * orbitals)
    hist_flat = lesser.reshape(rows_dev * orbitals, cols_dev * orbitals)
    propagator = jnp.eye(orbitals, dtype=F32) - STEP_SIZE * hamiltonian
    strength = (coupling * coupling)[:, None, :]
    current = first_row
    for section in range(greater_rows.shape[0]):
        greater = greater_rows[section]
        sigma_less = -strength * current * current * greater
        sigma_ret = -strength * greater * greater * current - sigma_less
        active = (row_times < step_index[0] + section).astype(F32)
        ret_flat = (sigma_ret * active[None, :, None]).reshape(orbitals, rows_dev * orbitals)
        less_flat = sigma_less.reshape(orbitals, rows_dev * orbitals)
        memory = jnp.dot(ret_flat, hist_flat, precision=PRECISE, preferred_element_type=F32)
        memory = memory + jnp.dot(less_flat, adv_flat, precision=PRECISE, preferred_element_type=F32)
        share = lax.psum_scatter(memory.reshape(orbitals, cols_dev, orbitals), "col", scatter_dimension=0, tiled=True)
        spread = lax.all_gather(share, "hist", axis=1, tiled=True)
        memory_block = lax.all_to_all(spread, "col", split_axis=1, concat_axis=0, tiled=True)
        moved = jnp.einsum("ik,ksj->isj", propagator, current, precision=PRECISE)
        current = moved - STEP_SIZE * memory_block
    return current


def solution(mesh):
    hist, cols = mesh.shape["hist"], mesh.shape["col"]

    def on_device(lesser, *rest):
        rows_dev, _, cols_dev, _ = lesser.shape
        if cols == 2 and cols_dev == 1 and hist == 2 * rows_dev and hist & (hist - 1) == 0 and rows_dev > 1:
            return in_pairs(hist, lesser, *rest)
        return in_general(lesser, *rest)

    in_specs = (
        P("col", None, "hist", None),
        P("col", None, "hist", None),
        P(None, "col", None),
        P(None, None, "col", None),
        P(),
        P(),
        P("hist"),
        P(),
    )
    return jax.shard_map(on_device, mesh=mesh, in_specs=in_specs, out_specs=P(None, "col", None), check_vma=False)
```

```python
import functools

import jax
import jax.numpy as jnp
from jax import lax
from jax.experimental import pallas as pl
from jax.experimental.pallas import tpu as pltpu
from jax.sharding import PartitionSpec as P

STEP_SIZE = 0.2
PRECISE = lax.Precision.HIGHEST
BF16 = jnp.bfloat16
F32 = jnp.float32
VMEM_BYTES = 12 * 2**20


def split(x):
    high = x.astype(BF16)
    return high, (x - high.astype(F32)).astype(BF16)


def tall(x):
    return jnp.concatenate(split(x), axis=0)


def wide(x):
    return jnp.concatenate(split(x), axis=1)


def product(rows, columns):
    m, n = rows.shape[0] // 2, columns.shape[1] // 2
    both = jnp.dot(rows, columns, preferred_element_type=F32)
    return both[:m, :n] + (both[:m, n:] + both[m:, :n])


def places(rows_dev):
    hist_pos = lax.axis_index("hist")
    return lax.rem(hist_pos, rows_dev), lax.rem(hist_pos, 2), lax.axis_index("col")


def slots(rows_dev, late):
    pairs = range(2, rows_dev - 2, 2) if late else (0, rows_dev - 2)
    return [pair + j for pair in pairs for j in range(2)]


def every(first, s, half, rows_dev):
    return pl.ds(first * rows_dev + s, half, stride=rows_dev)


def sigmas(section, rows_dev, half, late, cur, g_ref, g_first, active_ref, strength_ref, sigma_ref):
    n = 2 * half
    own_row, core, _ = places(rows_dev)
    strength = strength_ref[...]
    near = slots(rows_dev, late)
    for p, slot in enumerate(near):
        s = jnp.bitwise_xor(own_row, slot)
        x = cur[p]
        g = g_ref[every(g_first + core * half, s, half, rows_dev), :]
        u = strength * x * g
        less = -(u * x)
        ret = (u * x - u * g) * active_ref[pl.ds(section * rows_dev + s, 1), :]
        for where, value in ((p, ret), (len(near) + p, less)):
            sigma_ref[:, where * n : (where + 1) * n] = tall(value)


def split_tables(rows_dev, n, cutoff, lesser_ref, adv_ref, *wide_refs):
    own_row, _, col_pos = places(rows_dev)
    for late, wide_ref in enumerate(wide_refs):
        near = slots(rows_dev, late)
        for p, slot in enumerate(near):
            s = jnp.bitwise_xor(own_row, slot)
            inside = jnp.where(col_pos * rows_dev + s < cutoff, 1.0, 0.0).astype(F32)
            rows = pl.ds(pl.multiple_of(s * n, n), n)
            wide_ref[p * n : (p + 1) * n, :] = wide(lesser_ref[rows, :])
            where = (len(near) + p) * n
            wide_ref[where : where + n, :] = wide(adv_ref[rows, :] * inside)


def turn(half, step, ham_ref, near_ref, part_ref, far_ref, *rest):
    turned_ref = rest[-1]
    if step:
        own_ref, swapped_ref, new_ref = rest[:3]
        for j in range(2):
            new_ref[j, :half, :] = near_ref[j, :half, :] - STEP_SIZE * own_ref[j * half : (j + 1) * half, :]
            new_ref[j, half:, :] = near_ref[j, half:, :] - STEP_SIZE * swapped_ref[(1 - j) * half : (2 - j) * half, :]
        near_ref = new_ref
    for j in range(2):
        rows = slice(j * half, (j + 1) * half)
        turned_ref[rows, :] = product(ham_ref[...], wide(near_ref[j])) + (part_ref[rows, :] - far_ref[rows, :])


def store(rows_dev, half, parts, part_ref, far_ref):
    reads_own = lax.div(lax.axis_index("hist"), rows_dev) == lax.axis_index("col")
    for j, part in enumerate(parts):
        part_ref[j * half : (j + 1) * half, :] = part
        far_ref[j * half : (j + 1) * half, :] = jnp.where(reads_own, 0.0, part)


def first_kernel(rows_dev, half, steps, limits_ref, lesser_hbm, adv_hbm, first_hbm, greater_hbm, coup_hbm, ham_hbm,
                 cur_ref, late_cur_ref, wide_ref, late_wide_ref, active_ref, strength_ref, ham_ref, near_ref, sigma_ref, late_sigma_ref, own_ref,
                 lesser_ref, adv_ref, first_ref, g_ref, h_ref, sems):
    n = 2 * half
    own_row, core, col_pos = places(rows_dev)
    mine, other = core * half, (1 - core) * half
    rows = pl.ds(pl.multiple_of(mine, half), half)
    copies = [
        pltpu.make_async_copy(source, target, sems.at[k])
        for k, (source, target) in enumerate((
            (coup_hbm.at[rows], strength_ref),
            (ham_hbm.at[rows], h_ref),
            (first_hbm, first_ref),
            (greater_hbm.at[pl.ds(0, rows_dev * n)], g_ref),
            (lesser_hbm, lesser_ref),
            (adv_hbm, adv_ref),
        ))
    ]
    for copy in copies:
        copy.start()
    start, cutoff = limits_ref[0:1, :], limits_ref[1:2, :]
    for q in range(steps):
        for s in range(rows_dev):
            active_ref[q * rows_dev + s : q * rows_dev + s + 1, :] = jnp.where(
                col_pos * rows_dev + s < start + q, 1.0, 0.0
            ).astype(F32)
    for copy in copies[:4]:
        copy.wait()
    strength_ref[...] = strength_ref[...] * strength_ref[...]
    ham = h_ref[...]
    ham = tall(jnp.where(core == 0, ham, pltpu.roll(ham, half, 1)))
    ham_ref[...] = ham
    for late, (c_ref, s_ref) in enumerate(((cur_ref, sigma_ref), (late_cur_ref, late_sigma_ref))):
        for p, slot in enumerate(slots(rows_dev, late)):
            c_ref[p] = first_ref[every(mine, jnp.bitwise_xor(own_row, slot), half, rows_dev), :]
        sigmas(0, rows_dev, half, late, c_ref, g_ref, 0, active_ref, strength_ref, s_ref)
    for j in range(2):
        s = jnp.bitwise_xor(own_row, j)
        near_ref[j, :half, :] = first_ref[every(mine, s, half, rows_dev), :]
        near_ref[j, half:, :] = first_ref[every(other, s, half, rows_dev), :]
    for copy in copies[4:]:
        copy.wait()
    split_tables(rows_dev, n, cutoff, lesser_ref, adv_ref, wide_ref, late_wide_ref)
    own_ref[...] = product(sigma_ref[...], wide_ref[...]) + product(late_sigma_ref[...], late_wide_ref[...])


def second_kernel(rows_dev, half, limits_ref, lesser_ref, adv_ref, sigma_ref, late_sigma_ref, own_ref, wide_ref, late_wide_ref, part_ref, far_ref):
    split_tables(rows_dev, 2 * half, limits_ref[1:2, :], lesser_ref, adv_ref, wide_ref, late_wide_ref)
    other = product(sigma_ref[...], wide_ref[...]) + product(late_sigma_ref[...], late_wide_ref[...])
    store(rows_dev, half, (own_ref[...], other), part_ref, far_ref)


def update(prev_ref, pieces, cur_ref, half):
    for k, piece in enumerate(pieces):
        for j in range(2):
            cur_ref[2 * k + j] = prev_ref[2 * k + j] - STEP_SIZE * piece[j * half : (j + 1) * half, :]


def early_kernel(section, rows_dev, half, prev_ref, greater_ref, active_ref, strength_ref, own_wide_ref, other_wide_ref, *rest):
    pieces, (cur_ref, part_ref, sigma_ref) = rest[:2], rest[2:]
    update(prev_ref, pieces, cur_ref, half)
    sigmas(section, rows_dev, half, 0, cur_ref, greater_ref, section * 2 * half, active_ref, strength_ref, sigma_ref)
    part_ref[:half, :] = product(sigma_ref[...], own_wide_ref[...])
    part_ref[half:, :] = product(sigma_ref[...], other_wide_ref[...])


def late_kernel(section, rows_dev, half, prev_ref, greater_ref, active_ref, strength_ref, own_wide_ref, other_wide_ref, early_ref, *rest):
    count = rows_dev // 2 - 2
    pieces, (cur_ref, part_ref, far_ref, sigma_ref) = rest[:count], rest[count:]
    update(prev_ref, pieces, cur_ref, half)
    sigmas(section, rows_dev, half, 1, cur_ref, greater_ref, section * 2 * half, active_ref, strength_ref, sigma_ref)
    parts = [product(sigma_ref[...], table[...]) for table in (own_wide_ref, other_wide_ref)]
    parts = [part + early_ref[j * half : (j + 1) * half, :] for j, part in enumerate(parts)]
    store(rows_dev, half, parts, part_ref, far_ref)


def last_kernel(rows_dev, half, *refs):
    count = rows_dev // 2
    own_row, core, _ = places(rows_dev)
    out_hbm, out_ref, sems = refs[-3:]
    copies = []
    for away in range(2):
        prevs, pieces = refs[2 * away : 2 * away + 2], refs[4 + away * count : 4 + (away + 1) * count]
        side = jnp.bitwise_xor(core, away) * half
        for late, prev_ref in enumerate(prevs):
            for p, slot in enumerate(slots(rows_dev, late)):
                s = jnp.bitwise_xor(own_row, slot ^ away)
                piece = pieces[slot // 2]
                new = prev_ref[p] - STEP_SIZE * piece[slot % 2 * half : (slot % 2 + 1) * half, :]
                out_ref[every(side, s, half, rows_dev), :] = new
        flat = pl.ds(pl.multiple_of(side * rows_dev, half * rows_dev), half * rows_dev)
        copies.append(pltpu.make_async_copy(out_ref.at[flat], out_hbm.at[flat], sems.at[away]))
        copies[-1].start()
    for copy in copies:
        copy.wait()


def call(kernel, ins, outs, scratch, name):
    return pl.pallas_call(
        kernel,
        out_shape=[shape for shape, _ in outs],
        in_specs=[pl.BlockSpec(memory_space=space) for space in ins],
        out_specs=[pl.BlockSpec(memory_space=space) for _, space in outs],
        scratch_shapes=scratch,
        compiler_params=pltpu.CompilerParams(vmem_limit_bytes=VMEM_BYTES),
        name=name,
    )


def in_pairs(hist, lesser, advanced, first_row, greater_rows, hamiltonian, coupling, cutoff, step_index):
    rows_dev, n = lesser.shape[:2]
    steps, half = greater_rows.shape[0], n // 2
    flat = (rows_dev * n, n)
    shape, vmem, hbm = jax.ShapeDtypeStruct, pltpu.VMEM, pltpu.HBM

    def at(h, c):
        return h * 2 + c

    def block(h):
        return h // rows_dev

    def moved(x, pairs):
        return lax.ppermute(x, ("hist", "col"), pairs)

    def flip(x, bits):
        return moved(x, [(at(h, c), at(h ^ bits, c)) for h in range(hist) for c in range(2)])

    cycle = [(at(h, 1 - block(h)), at(h, block(h))) for h in range(hist)]
    cycle += [(at(h, block(h)), at(h ^ rows_dev, block(h))) for h in range(hist)]
    across = [(at(h, 1 - block(h)), at(h ^ rows_dev, block(h))) for h in range(hist)]
    across += [(at(h, block(h)), at(h ^ 1, block(h))) for h in range(hist)]

    def exchange(part, far, turned):
        own = moved(part, cycle) + moved(far, across) + turned
        return [own, flip(own, 1)] + [flip(own, bits) for bits in range(2, rows_dev, 2)]

    def out(dims, kind=F32):
        return shape(dims, kind), vmem

    greater = greater_rows.reshape(steps * rows_dev * n, n)
    tables = lesser.reshape(flat), advanced.reshape(flat)
    limits = jnp.broadcast_to(jnp.concatenate([step_index, cutoff])[:, None], (2, n))
    near_out = out((2, n, n))
    few, rest = 4, rows_dev - 4
    cur_outs = [out((count, half, n)) for count in (few, rest)]
    wide_outs = [out((2 * count * n, 2 * n), BF16) for count in (few, rest)]
    sigma_outs = [out((n, 2 * count * n), BF16) for count in (few, rest)]
    pair_out = out((n, n))
    *currents, own_wide, own_late_wide, active, strength, ham, near, sigma, late_sigma, own_part = call(
        functools.partial(first_kernel, rows_dev, half, steps),
        [vmem] + [hbm] * 6,
        [*cur_outs, *wide_outs, out((steps * rows_dev, n)), out((half, n)), out((n, n), BF16), near_out, *sigma_outs, out((half, n))],
        [vmem(flat, F32)] * 4 + [vmem((half, n), F32), pltpu.SemaphoreType.DMA((6,))],
        "first_step",
    )(limits, *[
        pltpu.with_memory_space_constraint(x, hbm)
        for x in (*tables, first_row.reshape(flat), greater, coupling, hamiltonian)
    ])
    other_wide, other_late_wide, part, far = call(
        functools.partial(second_kernel, rows_dev, half),
        [vmem] * 6, [*wide_outs, pair_out, pair_out], [], "first_step_other",
    )(flip(limits, 1), *[flip(x, 1) for x in tables], sigma, late_sigma, own_part)
    swap = []
    for section in range(1, steps + 1):
        *new, turned = call(
            functools.partial(turn, half, len(swap)), [vmem] * (4 + len(swap)), [near_out] * (len(swap) // 2) + [pair_out], [], "turn",
        )(ham, near, part, far, *swap)
        near = new[0] if new else near
        own, swapped, *others = exchange(part, far, turned)
        swap = [own, swapped]
        if section == steps:
            break
        given = greater, active, strength
        early, part = call(
            functools.partial(early_kernel, section, rows_dev, half),
            [vmem] * 8, [cur_outs[0], pair_out], [vmem(*x) for x in [((n, 2 * few * n), BF16)]], "next_step_early",
        )(currents[0], *given, own_wide, other_wide, own, others[-1])
        late, part, far = call(
            functools.partial(late_kernel, section, rows_dev, half),
            [vmem] * (7 + len(others) - 1), [cur_outs[1], pair_out, pair_out], [vmem((n, 2 * rest * n), BF16)], "next_step",
        )(currents[1], *given, own_late_wide, other_late_wide, part, *others[:-1])
        currents = [early, late]
    pieces = [own] + others
    final = call(
        functools.partial(last_kernel, rows_dev, half),
        [vmem] * (4 + rows_dev), [(shape(flat, F32), hbm)], [vmem(flat, F32), pltpu.SemaphoreType.DMA((2,))], "last_step",
    )(*currents, *[flip(x, 1) for x in currents], *pieces, swapped, *[flip(x, 1) for x in others])[0]
    return final.reshape(first_row.shape)


def in_general(lesser, advanced, first_row, greater_rows, hamiltonian, coupling, cutoff, step_index):
    rows_dev, orbitals, cols_dev, _ = lesser.shape
    row_times = lax.axis_index("col") * rows_dev + jnp.arange(rows_dev, dtype=jnp.int32)
    inside = (row_times[:, None] < cutoff[None, :]).astype(F32)
    adv_flat = (advanced * inside[:, None, :, None]).reshape(rows_dev * orbitals, cols_dev * orbitals)
    hist_flat = lesser.reshape(rows_dev * orbitals, cols_dev * orbitals)
    propagator = jnp.eye(orbitals, dtype=F32) - STEP_SIZE * hamiltonian
    strength = (coupling * coupling)[:, None, :]
    current = first_row
    for section in range(greater_rows.shape[0]):
        greater = greater_rows[section]
        sigma_less = -strength * current * current * greater
        sigma_ret = -strength * greater * greater * current - sigma_less
        active = (row_times < step_index[0] + section).astype(F32)
        ret_flat = (sigma_ret * active[None, :, None]).reshape(orbitals, rows_dev * orbitals)
        less_flat = sigma_less.reshape(orbitals, rows_dev * orbitals)
        memory = jnp.dot(ret_flat, hist_flat, precision=PRECISE, preferred_element_type=F32)
        memory = memory + jnp.dot(less_flat, adv_flat, precision=PRECISE, preferred_element_type=F32)
        share = lax.psum_scatter(memory.reshape(orbitals, cols_dev, orbitals), "col", scatter_dimension=0, tiled=True)
        spread = lax.all_gather(share, "hist", axis=1, tiled=True)
        memory_block = lax.all_to_all(spread, "col", split_axis=1, concat_axis=0, tiled=True)
        moved = jnp.einsum("ik,ksj->isj", propagator, current, precision=PRECISE)
        current = moved - STEP_SIZE * memory_block
    return current


def solution(mesh):
    hist, cols = mesh.shape["hist"], mesh.shape["col"]

    def on_device(lesser, *rest):
        rows_dev, _, cols_dev, _ = lesser.shape
        if cols == 2 and cols_dev == 1 and hist == 2 * rows_dev and hist & (hist - 1) == 0 and rows_dev > 4:
            return in_pairs(hist, lesser, *rest)
        return in_general(lesser, *rest)

    in_specs = (
        P("col", None, "hist", None),
        P("col", None, "hist", None),
        P(None, "col", None),
        P(None, None, "col", None),
        P(),
        P(),
        P("hist"),
        P(),
    )
    return jax.shard_map(on_device, mesh=mesh, in_specs=in_specs, out_specs=P(None, "col", None), check_vma=False)
```

```python
import functools

import jax
import jax.numpy as jnp
from jax import lax
from jax.experimental import pallas as pl
from jax.experimental.pallas import tpu as pltpu
from jax.sharding import PartitionSpec as P

STEP_SIZE = 0.2
PRECISE = lax.Precision.HIGHEST
BF16 = jnp.bfloat16
F32 = jnp.float32
VMEM_BYTES = 12 * 2**20


def split(x):
    high = x.astype(BF16)
    return high, (x - high.astype(F32)).astype(BF16)


def tall(x):
    return jnp.concatenate(split(x), axis=0)


def wide(x):
    return jnp.concatenate(split(x), axis=1)


def product(rows, columns):
    m, n = rows.shape[0] // 2, columns.shape[1] // 2
    both = jnp.dot(rows, columns, preferred_element_type=F32)
    return both[:m, :n] + (both[:m, n:] + both[m:, :n])


def places(rows_dev):
    hist_pos = lax.axis_index("hist")
    return lax.rem(hist_pos, rows_dev), lax.rem(hist_pos, 2), lax.axis_index("col")


def slots(rows_dev, late):
    pairs = range(2, rows_dev - 2, 2) if late else (0, rows_dev - 2)
    return [pair + j for pair in pairs for j in range(2)]


def every(first, s, half, rows_dev):
    return pl.ds(first * rows_dev + s, half, stride=rows_dev)


def sigmas(section, rows_dev, half, late, cur, g_ref, g_first, active_ref, strength_ref, sigma_ref):
    n = 2 * half
    own_row, core, _ = places(rows_dev)
    strength = strength_ref[...]
    near = slots(rows_dev, late)
    for p, slot in enumerate(near):
        s = jnp.bitwise_xor(own_row, slot)
        x = cur[p]
        g = g_ref[every(g_first + core * half, s, half, rows_dev), :]
        u = strength * x * g
        less = -(u * x)
        ret = (u * x - u * g) * active_ref[pl.ds(section * rows_dev + s, 1), :]
        for where, value in ((p, ret), (len(near) + p, less)):
            sigma_ref[:, where * n : (where + 1) * n] = tall(value)


def split_tables(rows_dev, n, cutoff, lesser_ref, adv_ref, *wide_refs):
    own_row, _, col_pos = places(rows_dev)
    for late, wide_ref in enumerate(wide_refs):
        near = slots(rows_dev, late)
        for p, slot in enumerate(near):
            s = jnp.bitwise_xor(own_row, slot)
            inside = jnp.where(col_pos * rows_dev + s < cutoff, 1.0, 0.0).astype(F32)
            rows = pl.ds(pl.multiple_of(s * n, n), n)
            wide_ref[p * n : (p + 1) * n, :] = wide(lesser_ref[rows, :])
            where = (len(near) + p) * n
            wide_ref[where : where + n, :] = wide(adv_ref[rows, :] * inside)


def turn(half, step, ham_ref, near_ref, part_ref, far_ref, *rest):
    turned_ref = rest[-1]
    if step:
        own_ref, swapped_ref, new_ref = rest[:3]
        for j in range(2):
            new_ref[j, :half, :] = near_ref[j, :half, :] - STEP_SIZE * own_ref[j * half : (j + 1) * half, :]
            new_ref[j, half:, :] = near_ref[j, half:, :] - STEP_SIZE * swapped_ref[(1 - j) * half : (2 - j) * half, :]
        near_ref = new_ref
    for j in range(2):
        rows = slice(j * half, (j + 1) * half)
        turned_ref[rows, :] = product(ham_ref[...], wide(near_ref[j])) + (part_ref[rows, :] - far_ref[rows, :])


def store(rows_dev, half, parts, part_ref, far_ref):
    reads_own = lax.div(lax.axis_index("hist"), rows_dev) == lax.axis_index("col")
    for j, part in enumerate(parts):
        part_ref[j * half : (j + 1) * half, :] = part
        far_ref[j * half : (j + 1) * half, :] = jnp.where(reads_own, 0.0, part)


def first_kernel(rows_dev, half, steps, limits_ref, lesser_hbm, adv_hbm, first_hbm, greater_hbm, coup_hbm, ham_hbm,
                 cur_ref, late_cur_ref, wide_ref, late_wide_ref, active_ref, strength_ref, ham_ref, near_ref, sigma_ref, late_sigma_ref, own_ref,
                 lesser_ref, adv_ref, first_ref, g_ref, h_ref, sems):
    n = 2 * half
    own_row, core, col_pos = places(rows_dev)
    mine, other = core * half, (1 - core) * half
    rows = pl.ds(pl.multiple_of(mine, half), half)
    copies = [
        pltpu.make_async_copy(source, target, sems.at[k])
        for k, (source, target) in enumerate((
            (coup_hbm.at[rows], strength_ref),
            (ham_hbm.at[rows], h_ref),
            (first_hbm, first_ref),
            (greater_hbm.at[pl.ds(0, rows_dev * n)], g_ref),
            (lesser_hbm, lesser_ref),
            (adv_hbm, adv_ref),
        ))
    ]
    for copy in copies:
        copy.start()
    start, cutoff = limits_ref[0:1, :], limits_ref[1:2, :]
    for q in range(steps):
        for s in range(rows_dev):
            active_ref[q * rows_dev + s : q * rows_dev + s + 1, :] = jnp.where(
                col_pos * rows_dev + s < start + q, 1.0, 0.0
            ).astype(F32)
    for copy in copies[:4]:
        copy.wait()
    strength_ref[...] = strength_ref[...] * strength_ref[...]
    ham = h_ref[...]
    ham = tall(jnp.where(core == 0, ham, pltpu.roll(ham, half, 1)))
    ham_ref[...] = ham
    for late, (c_ref, s_ref) in enumerate(((cur_ref, sigma_ref), (late_cur_ref, late_sigma_ref))):
        for p, slot in enumerate(slots(rows_dev, late)):
            c_ref[p] = first_ref[every(mine, jnp.bitwise_xor(own_row, slot), half, rows_dev), :]
        sigmas(0, rows_dev, half, late, c_ref, g_ref, 0, active_ref, strength_ref, s_ref)
    for j in range(2):
        s = jnp.bitwise_xor(own_row, j)
        near_ref[j, :half, :] = first_ref[every(mine, s, half, rows_dev), :]
        near_ref[j, half:, :] = first_ref[every(other, s, half, rows_dev), :]
    for copy in copies[4:]:
        copy.wait()
    split_tables(rows_dev, n, cutoff, lesser_ref, adv_ref, wide_ref, late_wide_ref)
    own_ref[...] = product(sigma_ref[...], wide_ref[...]) + product(late_sigma_ref[...], late_wide_ref[...])


def second_kernel(rows_dev, half, limits_ref, lesser_ref, adv_ref, sigma_ref, late_sigma_ref, own_ref, wide_ref, late_wide_ref, part_ref, far_ref):
    split_tables(rows_dev, 2 * half, limits_ref[1:2, :], lesser_ref, adv_ref, wide_ref, late_wide_ref)
    other = product(sigma_ref[...], wide_ref[...]) + product(late_sigma_ref[...], late_wide_ref[...])
    store(rows_dev, half, (own_ref[...], other), part_ref, far_ref)


def update(prev_ref, pieces, cur_ref, half):
    for k, piece in enumerate(pieces):
        for j in range(2):
            cur_ref[2 * k + j] = prev_ref[2 * k + j] - STEP_SIZE * piece[j * half : (j + 1) * half, :]


def early_kernel(section, rows_dev, half, prev_ref, greater_ref, active_ref, strength_ref, own_wide_ref, other_wide_ref, *rest):
    pieces, (cur_ref, part_ref, sigma_ref) = rest[:2], rest[2:]
    update(prev_ref, pieces, cur_ref, half)
    sigmas(section, rows_dev, half, 0, cur_ref, greater_ref, section * 2 * half, active_ref, strength_ref, sigma_ref)
    part_ref[:half, :] = product(sigma_ref[...], own_wide_ref[...])
    part_ref[half:, :] = product(sigma_ref[...], other_wide_ref[...])


def late_kernel(section, rows_dev, half, prev_ref, greater_ref, active_ref, strength_ref, own_wide_ref, other_wide_ref, early_ref, *rest):
    count = rows_dev // 2 - 2
    pieces, (cur_ref, part_ref, far_ref, sigma_ref) = rest[:count], rest[count:]
    update(prev_ref, pieces, cur_ref, half)
    sigmas(section, rows_dev, half, 1, cur_ref, greater_ref, section * 2 * half, active_ref, strength_ref, sigma_ref)
    parts = [product(sigma_ref[...], table[...]) for table in (own_wide_ref, other_wide_ref)]
    parts = [part + early_ref[j * half : (j + 1) * half, :] for j, part in enumerate(parts)]
    store(rows_dev, half, parts, part_ref, far_ref)


def last_kernel(rows_dev, half, away, *refs):
    own_row, core, _ = places(rows_dev)
    out_hbm, out_ref, sem = refs[-3:]
    prevs, pieces = refs[:2], refs[2 : 2 + rows_dev // 2]
    side = jnp.bitwise_xor(core, away) * half
    for late, prev_ref in enumerate(prevs):
        for p, slot in enumerate(slots(rows_dev, late)):
            s = jnp.bitwise_xor(own_row, slot ^ away)
            piece = pieces[slot // 2]
            new = prev_ref[p] - STEP_SIZE * piece[slot % 2 * half : (slot % 2 + 1) * half, :]
            out_ref[pl.ds(s, half, stride=rows_dev), :] = new
    flat = pl.ds(pl.multiple_of(side * rows_dev, half * rows_dev), half * rows_dev)
    copy = pltpu.make_async_copy(out_ref, out_hbm.at[flat], sem)
    copy.start()
    copy.wait()


def call(kernel, ins, outs, scratch, name, aliases={}):
    return pl.pallas_call(
        kernel,
        out_shape=[shape for shape, _ in outs],
        in_specs=[pl.BlockSpec(memory_space=space) for space in ins],
        out_specs=[pl.BlockSpec(memory_space=space) for _, space in outs],
        scratch_shapes=scratch,
        compiler_params=pltpu.CompilerParams(vmem_limit_bytes=VMEM_BYTES),
        name=name,
        input_output_aliases=aliases,
    )


def in_pairs(hist, lesser, advanced, first_row, greater_rows, hamiltonian, coupling, cutoff, step_index):
    rows_dev, n = lesser.shape[:2]
    steps, half = greater_rows.shape[0], n // 2
    flat = (rows_dev * n, n)
    shape, vmem, hbm = jax.ShapeDtypeStruct, pltpu.VMEM, pltpu.HBM

    def at(h, c):
        return h * 2 + c

    def block(h):
        return h // rows_dev

    def moved(x, pairs):
        return lax.ppermute(x, ("hist", "col"), pairs)

    def flip(x, bits):
        return moved(x, [(at(h, c), at(h ^ bits, c)) for h in range(hist) for c in range(2)])

    cycle = [(at(h, 1 - block(h)), at(h, block(h))) for h in range(hist)]
    cycle += [(at(h, block(h)), at(h ^ rows_dev, block(h))) for h in range(hist)]
    across = [(at(h, 1 - block(h)), at(h ^ rows_dev, block(h))) for h in range(hist)]
    across += [(at(h, block(h)), at(h ^ 1, block(h))) for h in range(hist)]

    def exchange(part, far, turned):
        own = moved(part, cycle) + moved(far, across) + turned
        return [own, flip(own, 1)] + [flip(own, bits) for bits in range(2, rows_dev, 2)]

    def out(dims, kind=F32):
        return shape(dims, kind), vmem

    greater = greater_rows.reshape(steps * rows_dev * n, n)
    tables = lesser.reshape(flat), advanced.reshape(flat)
    limits = jnp.broadcast_to(jnp.concatenate([step_index, cutoff])[:, None], (2, n))
    near_out = out((2, n, n))
    few, rest = 4, rows_dev - 4
    cur_outs = [out((count, half, n)) for count in (few, rest)]
    wide_outs = [out((2 * count * n, 2 * n), BF16) for count in (few, rest)]
    sigma_outs = [out((n, 2 * count * n), BF16) for count in (few, rest)]
    pair_out = out((n, n))
    *currents, own_wide, own_late_wide, active, strength, ham, near, sigma, late_sigma, own_part = call(
        functools.partial(first_kernel, rows_dev, half, steps),
        [vmem] + [hbm] * 6,
        [*cur_outs, *wide_outs, out((steps * rows_dev, n)), out((half, n)), out((n, n), BF16), near_out, *sigma_outs, out((half, n))],
        [vmem(flat, F32)] * 4 + [vmem((half, n), F32), pltpu.SemaphoreType.DMA((6,))],
        "first_step",
    )(limits, *[
        pltpu.with_memory_space_constraint(x, hbm)
        for x in (*tables, first_row.reshape(flat), greater, coupling, hamiltonian)
    ])
    other_wide, other_late_wide, part, far = call(
        functools.partial(second_kernel, rows_dev, half),
        [vmem] * 6, [*wide_outs, pair_out, pair_out], [], "first_step_other",
    )(flip(limits, 1), *[flip(x, 1) for x in tables], sigma, late_sigma, own_part)
    swap = []
    for section in range(1, steps + 1):
        *new, turned = call(
            functools.partial(turn, half, len(swap)), [vmem] * (4 + len(swap)), [near_out] * (len(swap) // 2) + [pair_out], [], "turn",
        )(ham, near, part, far, *swap)
        near = new[0] if new else near
        own, swapped, *others = exchange(part, far, turned)
        swap = [own, swapped]
        if section == steps:
            break
        given = greater, active, strength
        early, part = call(
            functools.partial(early_kernel, section, rows_dev, half),
            [vmem] * 8, [cur_outs[0], pair_out], [vmem(*x) for x in [((n, 2 * few * n), BF16)]], "next_step_early",
        )(currents[0], *given, own_wide, other_wide, own, others[-1])
        late, part, far = call(
            functools.partial(late_kernel, section, rows_dev, half),
            [vmem] * (7 + len(others) - 1), [cur_outs[1], pair_out, pair_out], [vmem((n, 2 * rest * n), BF16)], "next_step",
        )(currents[1], *given, own_late_wide, other_late_wide, part, *others[:-1])
        currents = [early, late]
    pieces = [own] + others
    final_out, stage = [(shape(flat, F32), hbm)], [vmem((half * rows_dev, n), F32), pltpu.SemaphoreType.DMA]
    final = call(
        functools.partial(last_kernel, rows_dev, half, 0), [vmem] * (2 + rows_dev // 2), final_out, stage, "last_step",
    )(*currents, *pieces)[0]
    final = call(
        functools.partial(last_kernel, rows_dev, half, 1),
        [vmem] * (2 + rows_dev // 2) + [hbm], final_out, stage, "last_step_other", {2 + rows_dev // 2: 0},
    )(*[flip(x, 1) for x in currents], swapped, *[flip(x, 1) for x in others], final)[0]
    return final.reshape(first_row.shape)


def in_general(lesser, advanced, first_row, greater_rows, hamiltonian, coupling, cutoff, step_index):
    rows_dev, orbitals, cols_dev, _ = lesser.shape
    row_times = lax.axis_index("col") * rows_dev + jnp.arange(rows_dev, dtype=jnp.int32)
    inside = (row_times[:, None] < cutoff[None, :]).astype(F32)
    adv_flat = (advanced * inside[:, None, :, None]).reshape(rows_dev * orbitals, cols_dev * orbitals)
    hist_flat = lesser.reshape(rows_dev * orbitals, cols_dev * orbitals)
    propagator = jnp.eye(orbitals, dtype=F32) - STEP_SIZE * hamiltonian
    strength = (coupling * coupling)[:, None, :]
    current = first_row
    for section in range(greater_rows.shape[0]):
        greater = greater_rows[section]
        sigma_less = -strength * current * current * greater
        sigma_ret = -strength * greater * greater * current - sigma_less
        active = (row_times < step_index[0] + section).astype(F32)
        ret_flat = (sigma_ret * active[None, :, None]).reshape(orbitals, rows_dev * orbitals)
        less_flat = sigma_less.reshape(orbitals, rows_dev * orbitals)
        memory = jnp.dot(ret_flat, hist_flat, precision=PRECISE, preferred_element_type=F32)
        memory = memory + jnp.dot(less_flat, adv_flat, precision=PRECISE, preferred_element_type=F32)
        share = lax.psum_scatter(memory.reshape(orbitals, cols_dev, orbitals), "col", scatter_dimension=0, tiled=True)
        spread = lax.all_gather(share, "hist", axis=1, tiled=True)
        memory_block = lax.all_to_all(spread, "col", split_axis=1, concat_axis=0, tiled=True)
        moved = jnp.einsum("ik,ksj->isj", propagator, current, precision=PRECISE)
        current = moved - STEP_SIZE * memory_block
    return current


def solution(mesh):
    hist, cols = mesh.shape["hist"], mesh.shape["col"]

    def on_device(lesser, *rest):
        rows_dev, _, cols_dev, _ = lesser.shape
        if cols == 2 and cols_dev == 1 and hist == 2 * rows_dev and hist & (hist - 1) == 0 and rows_dev > 4:
            return in_pairs(hist, lesser, *rest)
        return in_general(lesser, *rest)

    in_specs = (
        P("col", None, "hist", None),
        P("col", None, "hist", None),
        P(None, "col", None),
        P(None, None, "col", None),
        P(),
        P(),
        P("hist"),
        P(),
    )
    return jax.shard_map(on_device, mesh=mesh, in_specs=in_specs, out_specs=P(None, "col", None), check_vma=False)
```

```python
import functools

import jax
import jax.numpy as jnp
from jax import lax
from jax.experimental import pallas as pl
from jax.experimental.pallas import tpu as pltpu
from jax.sharding import PartitionSpec as P

STEP_SIZE = 0.2
PRECISE = lax.Precision.HIGHEST
BF16 = jnp.bfloat16
F32 = jnp.float32
VMEM_BYTES = 12 * 2**20


def split(x):
    high = x.astype(BF16)
    return high, (x - high.astype(F32)).astype(BF16)


def tall(x):
    return jnp.concatenate(split(x), axis=0)


def wide(x):
    return jnp.concatenate(split(x), axis=1)


def product(rows, columns):
    m, n = rows.shape[0] // 2, columns.shape[1] // 2
    both = jnp.dot(rows, columns, preferred_element_type=F32)
    return both[:m, :n] + (both[:m, n:] + both[m:, :n])


def places(rows_dev):
    hist_pos = lax.axis_index("hist")
    return lax.rem(hist_pos, rows_dev), lax.rem(hist_pos, 2), lax.axis_index("col")


def slots(rows_dev, late):
    pairs = range(2, rows_dev - 2, 2) if late else (0, rows_dev - 2)
    return [pair + j for pair in pairs for j in range(2)]


def every(first, s, half, rows_dev):
    return pl.ds(first * rows_dev + s, half, stride=rows_dev)


def sigmas(section, rows_dev, half, late, cur, g_ref, g_first, active_ref, strength_ref, sigma_ref):
    n = 2 * half
    own_row, core, _ = places(rows_dev)
    strength = strength_ref[...]
    near = slots(rows_dev, late)
    for p, slot in enumerate(near):
        s = jnp.bitwise_xor(own_row, slot)
        x = cur[p]
        g = g_ref[every(g_first + core * half, s, half, rows_dev), :]
        u = strength * x * g
        less = -(u * x)
        ret = (u * x - u * g) * active_ref[pl.ds(section * rows_dev + s, 1), :]
        for where, value in ((p, ret), (len(near) + p, less)):
            sigma_ref[:, where * n : (where + 1) * n] = tall(value)


def split_tables(rows_dev, n, cutoff, lesser_ref, adv_ref, *wide_refs):
    own_row, _, col_pos = places(rows_dev)
    for late, wide_ref in enumerate(wide_refs):
        near = slots(rows_dev, late)
        for p, slot in enumerate(near):
            s = jnp.bitwise_xor(own_row, slot)
            inside = jnp.where(col_pos * rows_dev + s < cutoff, 1.0, 0.0).astype(F32)
            rows = pl.ds(pl.multiple_of(s * n, n), n)
            wide_ref[p * n : (p + 1) * n, :] = wide(lesser_ref[rows, :])
            where = (len(near) + p) * n
            wide_ref[where : where + n, :] = wide(adv_ref[rows, :] * inside)


def turn(half, step, ham_ref, near_ref, part_ref, far_ref, *rest):
    turned_ref = rest[-1]
    if step:
        own_ref, swapped_ref, new_ref = rest[:3]
        for j in range(2):
            new_ref[j, :half, :] = near_ref[j, :half, :] - STEP_SIZE * own_ref[j * half : (j + 1) * half, :]
            new_ref[j, half:, :] = near_ref[j, half:, :] - STEP_SIZE * swapped_ref[(1 - j) * half : (2 - j) * half, :]
        near_ref = new_ref
    for j in range(2):
        rows = slice(j * half, (j + 1) * half)
        turned_ref[rows, :] = product(ham_ref[...], wide(near_ref[j])) + (part_ref[rows, :] - far_ref[rows, :])


def store(rows_dev, half, parts, part_ref, far_ref):
    reads_own = lax.div(lax.axis_index("hist"), rows_dev) == lax.axis_index("col")
    for j, part in enumerate(parts):
        part_ref[j * half : (j + 1) * half, :] = part
        far_ref[j * half : (j + 1) * half, :] = jnp.where(reads_own, 0.0, part)


def first_kernel(rows_dev, half, steps, limits_ref, lesser_hbm, adv_hbm, first_hbm, greater_hbm, coup_hbm, ham_hbm,
                 cur_ref, late_cur_ref, wide_ref, late_wide_ref, active_ref, strength_ref, ham_ref, near_ref, sigma_ref, late_sigma_ref, own_ref,
                 lesser_ref, adv_ref, first_ref, g_ref, h_ref, sems):
    n = 2 * half
    own_row, core, col_pos = places(rows_dev)
    mine, other = core * half, (1 - core) * half
    rows = pl.ds(pl.multiple_of(mine, half), half)
    copies = [
        pltpu.make_async_copy(source, target, sems.at[k])
        for k, (source, target) in enumerate((
            (coup_hbm.at[rows], strength_ref),
            (ham_hbm.at[rows], h_ref),
            (first_hbm, first_ref),
            (greater_hbm.at[pl.ds(0, rows_dev * n)], g_ref),
            (lesser_hbm, lesser_ref),
            (adv_hbm, adv_ref),
        ))
    ]
    for copy in copies:
        copy.start()
    start, cutoff = limits_ref[0:1, :], limits_ref[1:2, :]
    for q in range(steps):
        for s in range(rows_dev):
            active_ref[q * rows_dev + s : q * rows_dev + s + 1, :] = jnp.where(
                col_pos * rows_dev + s < start + q, 1.0, 0.0
            ).astype(F32)
    for copy in copies[:4]:
        copy.wait()
    strength_ref[...] = strength_ref[...] * strength_ref[...]
    ham = h_ref[...]
    ham = tall(jnp.where(core == 0, ham, pltpu.roll(ham, half, 1)))
    ham_ref[...] = ham
    for late, (c_ref, s_ref) in enumerate(((cur_ref, sigma_ref), (late_cur_ref, late_sigma_ref))):
        for p, slot in enumerate(slots(rows_dev, late)):
            c_ref[p] = first_ref[every(mine, jnp.bitwise_xor(own_row, slot), half, rows_dev), :]
        sigmas(0, rows_dev, half, late, c_ref, g_ref, 0, active_ref, strength_ref, s_ref)
    for j in range(2):
        s = jnp.bitwise_xor(own_row, j)
        near_ref[j, :half, :] = first_ref[every(mine, s, half, rows_dev), :]
        near_ref[j, half:, :] = first_ref[every(other, s, half, rows_dev), :]
    for copy in copies[4:]:
        copy.wait()
    split_tables(rows_dev, n, cutoff, lesser_ref, adv_ref, wide_ref, late_wide_ref)
    own_ref[...] = product(sigma_ref[...], wide_ref[...]) + product(late_sigma_ref[...], late_wide_ref[...])


def second_kernel(rows_dev, half, limits_ref, lesser_ref, adv_ref, sigma_ref, late_sigma_ref, own_ref, wide_ref, late_wide_ref, part_ref, far_ref):
    split_tables(rows_dev, 2 * half, limits_ref[1:2, :], lesser_ref, adv_ref, wide_ref, late_wide_ref)
    other = product(sigma_ref[...], wide_ref[...]) + product(late_sigma_ref[...], late_wide_ref[...])
    store(rows_dev, half, (own_ref[...], other), part_ref, far_ref)


def update(prev_ref, pieces, cur_ref, half):
    for k, piece in enumerate(pieces):
        for j in range(2):
            cur_ref[2 * k + j] = prev_ref[2 * k + j] - STEP_SIZE * piece[j * half : (j + 1) * half, :]


def early_kernel(section, rows_dev, half, prev_ref, greater_ref, active_ref, strength_ref, own_wide_ref, other_wide_ref, *rest):
    pieces, (cur_ref, part_ref, sigma_ref) = rest[:2], rest[2:]
    update(prev_ref, pieces, cur_ref, half)
    sigmas(section, rows_dev, half, 0, cur_ref, greater_ref, section * 2 * half, active_ref, strength_ref, sigma_ref)
    part_ref[:half, :] = product(sigma_ref[...], own_wide_ref[...])
    part_ref[half:, :] = product(sigma_ref[...], other_wide_ref[...])


def late_kernel(section, rows_dev, half, prev_ref, greater_ref, active_ref, strength_ref, own_wide_ref, other_wide_ref, early_ref, *rest):
    count = rows_dev // 2 - 2
    pieces, (cur_ref, part_ref, far_ref, sigma_ref) = rest[:count], rest[count:]
    update(prev_ref, pieces, cur_ref, half)
    sigmas(section, rows_dev, half, 1, cur_ref, greater_ref, section * 2 * half, active_ref, strength_ref, sigma_ref)
    parts = [product(sigma_ref[...], table[...]) for table in (own_wide_ref, other_wide_ref)]
    parts = [part + early_ref[j * half : (j + 1) * half, :] for j, part in enumerate(parts)]
    store(rows_dev, half, parts, part_ref, far_ref)


def last_kernel(rows_dev, half, *refs):
    count = rows_dev // 2
    own_row, core, _ = places(rows_dev)
    out_hbm, out_ref, sems = refs[-3:]
    copies = []
    for away in range(2):
        prevs, pieces = refs[2 * away : 2 * away + 2], refs[4 + away * count : 4 + (away + 1) * count]
        side = jnp.bitwise_xor(core, away) * half
        for late, prev_ref in enumerate(prevs):
            for p, slot in enumerate(slots(rows_dev, late)):
                s = jnp.bitwise_xor(own_row, slot ^ away)
                piece = pieces[slot // 2]
                new = prev_ref[p] - STEP_SIZE * piece[slot % 2 * half : (slot % 2 + 1) * half, :]
                out_ref[every(side, s, half, rows_dev), :] = new
        flat = pl.ds(pl.multiple_of(side * rows_dev, half * rows_dev), half * rows_dev)
        copies.append(pltpu.make_async_copy(out_ref.at[flat], out_hbm.at[flat], sems.at[away]))
        copies[-1].start()
    for copy in copies:
        copy.wait()


def call(kernel, ins, outs, scratch, name):
    return pl.pallas_call(
        kernel,
        out_shape=[shape for shape, _ in outs],
        in_specs=[pl.BlockSpec(memory_space=space) for space in ins],
        out_specs=[pl.BlockSpec(memory_space=space) for _, space in outs],
        scratch_shapes=scratch,
        compiler_params=pltpu.CompilerParams(vmem_limit_bytes=VMEM_BYTES),
        name=name,
    )


def in_pairs(hist, lesser, advanced, first_row, greater_rows, hamiltonian, coupling, cutoff, step_index):
    rows_dev, n = lesser.shape[:2]
    steps, half = greater_rows.shape[0], n // 2
    flat = (rows_dev * n, n)
    shape, vmem, hbm = jax.ShapeDtypeStruct, pltpu.VMEM, pltpu.HBM

    def at(h, c):
        return h * 2 + c

    def block(h):
        return h // rows_dev

    def moved(x, pairs):
        return lax.ppermute(x, ("hist", "col"), pairs)

    def flip(x, bits):
        return moved(x, [(at(h, c), at(h ^ bits, c)) for h in range(hist) for c in range(2)])

    cycle = [(at(h, 1 - block(h)), at(h, block(h))) for h in range(hist)]
    cycle += [(at(h, block(h)), at(h ^ rows_dev, block(h))) for h in range(hist)]
    across = [(at(h, 1 - block(h)), at(h ^ rows_dev, block(h))) for h in range(hist)]
    across += [(at(h, block(h)), at(h ^ 1, block(h))) for h in range(hist)]

    def exchange(part, far, turned):
        own = moved(part, cycle) + moved(far, across) + turned
        return [own, flip(own, 1)] + [flip(own, bits) for bits in range(2, rows_dev, 2)]

    def out(dims, kind=F32):
        return shape(dims, kind), vmem

    greater = greater_rows.reshape(steps * rows_dev * n, n)
    tables = lesser.reshape(flat), advanced.reshape(flat)
    limits = jnp.broadcast_to(jnp.concatenate([step_index, cutoff])[:, None], (2, n))
    near_out = out((2, n, n))
    few, rest = 4, rows_dev - 4
    cur_outs = [out((count, half, n)) for count in (few, rest)]
    wide_outs = [out((2 * count * n, 2 * n), BF16) for count in (few, rest)]
    sigma_outs = [out((n, 2 * count * n), BF16) for count in (few, rest)]
    pair_out = out((n, n))
    *currents, own_wide, own_late_wide, active, strength, ham, near, sigma, late_sigma, own_part = call(
        functools.partial(first_kernel, rows_dev, half, steps),
        [vmem] + [hbm] * 6,
        [*cur_outs, *wide_outs, out((steps * rows_dev, n)), out((half, n)), out((n, n), BF16), near_out, *sigma_outs, out((half, n))],
        [vmem(flat, F32)] * 4 + [vmem((half, n), F32), pltpu.SemaphoreType.DMA((6,))],
        "first_step",
    )(limits, *[
        pltpu.with_memory_space_constraint(x, hbm)
        for x in (*tables, first_row.reshape(flat), greater, coupling, hamiltonian)
    ])
    other_wide, other_late_wide, part, far = call(
        functools.partial(second_kernel, rows_dev, half),
        [vmem] * 6, [*wide_outs, pair_out, pair_out], [], "first_step_other",
    )(flip(limits, 1), *[flip(x, 1) for x in lax.optimization_barrier((limits, *tables))[1:]], sigma, late_sigma, own_part)
    swap = []
    for section in range(1, steps + 1):
        *new, turned = call(
            functools.partial(turn, half, len(swap)), [vmem] * (4 + len(swap)), [near_out] * (len(swap) // 2) + [pair_out], [], "turn",
        )(ham, near, part, far, *swap)
        near = new[0] if new else near
        own, swapped, *others = exchange(part, far, turned)
        swap = [own, swapped]
        if section == steps:
            break
        given = greater, active, strength
        early, part = call(
            functools.partial(early_kernel, section, rows_dev, half),
            [vmem] * 8, [cur_outs[0], pair_out], [vmem(*x) for x in [((n, 2 * few * n), BF16)]], "next_step_early",
        )(currents[0], *given, own_wide, other_wide, own, others[-1])
        late, part, far = call(
            functools.partial(late_kernel, section, rows_dev, half),
            [vmem] * (7 + len(others) - 1), [cur_outs[1], pair_out, pair_out], [vmem((n, 2 * rest * n), BF16)], "next_step",
        )(currents[1], *given, own_late_wide, other_late_wide, part, *others[:-1])
        currents = [early, late]
    pieces = [own] + others
    final = call(
        functools.partial(last_kernel, rows_dev, half),
        [vmem] * (4 + rows_dev), [(shape(flat, F32), hbm)], [vmem(flat, F32), pltpu.SemaphoreType.DMA((2,))], "last_step",
    )(*currents, *[flip(x, 1) for x in currents], *pieces, swapped, *[flip(x, 1) for x in others])[0]
    return final.reshape(first_row.shape)


def in_general(lesser, advanced, first_row, greater_rows, hamiltonian, coupling, cutoff, step_index):
    rows_dev, orbitals, cols_dev, _ = lesser.shape
    row_times = lax.axis_index("col") * rows_dev + jnp.arange(rows_dev, dtype=jnp.int32)
    inside = (row_times[:, None] < cutoff[None, :]).astype(F32)
    adv_flat = (advanced * inside[:, None, :, None]).reshape(rows_dev * orbitals, cols_dev * orbitals)
    hist_flat = lesser.reshape(rows_dev * orbitals, cols_dev * orbitals)
    propagator = jnp.eye(orbitals, dtype=F32) - STEP_SIZE * hamiltonian
    strength = (coupling * coupling)[:, None, :]
    current = first_row
    for section in range(greater_rows.shape[0]):
        greater = greater_rows[section]
        sigma_less = -strength * current * current * greater
        sigma_ret = -strength * greater * greater * current - sigma_less
        active = (row_times < step_index[0] + section).astype(F32)
        ret_flat = (sigma_ret * active[None, :, None]).reshape(orbitals, rows_dev * orbitals)
        less_flat = sigma_less.reshape(orbitals, rows_dev * orbitals)
        memory = jnp.dot(ret_flat, hist_flat, precision=PRECISE, preferred_element_type=F32)
        memory = memory + jnp.dot(less_flat, adv_flat, precision=PRECISE, preferred_element_type=F32)
        share = lax.psum_scatter(memory.reshape(orbitals, cols_dev, orbitals), "col", scatter_dimension=0, tiled=True)
        spread = lax.all_gather(share, "hist", axis=1, tiled=True)
        memory_block = lax.all_to_all(spread, "col", split_axis=1, concat_axis=0, tiled=True)
        moved = jnp.einsum("ik,ksj->isj", propagator, current, precision=PRECISE)
        current = moved - STEP_SIZE * memory_block
    return current


def solution(mesh):
    hist, cols = mesh.shape["hist"], mesh.shape["col"]

    def on_device(lesser, *rest):
        rows_dev, _, cols_dev, _ = lesser.shape
        if cols == 2 and cols_dev == 1 and hist == 2 * rows_dev and hist & (hist - 1) == 0 and rows_dev > 4:
            return in_pairs(hist, lesser, *rest)
        return in_general(lesser, *rest)

    in_specs = (
        P("col", None, "hist", None),
        P("col", None, "hist", None),
        P(None, "col", None),
        P(None, None, "col", None),
        P(),
        P(),
        P("hist"),
        P(),
    )
    return jax.shard_map(on_device, mesh=mesh, in_specs=in_specs, out_specs=P(None, "col", None), check_vma=False)
```

```python
import functools

import jax
import jax.numpy as jnp
from jax import lax
from jax.experimental import pallas as pl
from jax.experimental.pallas import tpu as pltpu
from jax.sharding import PartitionSpec as P

STEP_SIZE = 0.2
PRECISE = lax.Precision.HIGHEST
BF16 = jnp.bfloat16
F32 = jnp.float32
VMEM_BYTES = 12 * 2**20


def split(x):
    high = x.astype(BF16)
    return high, (x - high.astype(F32)).astype(BF16)


def tall(x):
    return jnp.concatenate(split(x), axis=0)


def wide(x):
    return jnp.concatenate(split(x), axis=1)


def product(rows, columns):
    m, n = rows.shape[0] // 2, columns.shape[1] // 2
    both = jnp.dot(rows, columns, preferred_element_type=F32)
    return both[:m, :n] + (both[:m, n:] + both[m:, :n])


def places(rows_dev):
    hist_pos = lax.axis_index("hist")
    return lax.rem(hist_pos, rows_dev), lax.rem(hist_pos, 2), lax.axis_index("col")


def slots(rows_dev, late):
    pairs = range(2, rows_dev - 2, 2) if late else (0, rows_dev - 2)
    return [pair + j for pair in pairs for j in range(2)]


def every(first, s, half, rows_dev):
    return pl.ds(first * rows_dev + s, half, stride=rows_dev)


def sigmas(section, rows_dev, half, late, cur, g_ref, g_first, active_ref, strength_ref, sigma_ref):
    n = 2 * half
    own_row, core, _ = places(rows_dev)
    strength = strength_ref[...]
    near = slots(rows_dev, late)
    for p, slot in enumerate(near):
        s = jnp.bitwise_xor(own_row, slot)
        x = cur[p]
        g = g_ref[every(g_first + core * half, s, half, rows_dev), :]
        u = strength * x * g
        less = -(u * x)
        ret = (u * x - u * g) * active_ref[pl.ds(section * rows_dev + s, 1), :]
        for where, value in ((p, ret), (len(near) + p, less)):
            sigma_ref[:, where * n : (where + 1) * n] = tall(value)


def split_tables(rows_dev, n, cutoff, lesser_ref, adv_ref, *wide_refs):
    own_row, _, col_pos = places(rows_dev)
    for late, wide_ref in enumerate(wide_refs):
        near = slots(rows_dev, late)
        for p, slot in enumerate(near):
            s = jnp.bitwise_xor(own_row, slot)
            inside = jnp.where(col_pos * rows_dev + s < cutoff, 1.0, 0.0).astype(F32)
            rows = pl.ds(pl.multiple_of(s * n, n), n)
            wide_ref[p * n : (p + 1) * n, :] = wide(lesser_ref[rows, :])
            where = (len(near) + p) * n
            wide_ref[where : where + n, :] = wide(adv_ref[rows, :] * inside)


def turn(half, step, ham_ref, near_ref, part_ref, far_ref, *rest):
    turned_ref = rest[-1]
    if step:
        own_ref, swapped_ref, new_ref = rest[:3]
        for j in range(2):
            new_ref[j, :half, :] = near_ref[j, :half, :] - STEP_SIZE * own_ref[j * half : (j + 1) * half, :]
            new_ref[j, half:, :] = near_ref[j, half:, :] - STEP_SIZE * swapped_ref[(1 - j) * half : (2 - j) * half, :]
        near_ref = new_ref
    for j in range(2):
        rows = slice(j * half, (j + 1) * half)
        turned_ref[rows, :] = product(ham_ref[...], wide(near_ref[j])) + (part_ref[rows, :] - far_ref[rows, :])


def turn_last(half, *refs):
    turn(half, 2, *refs[:6], refs[7], refs[6])


def store(rows_dev, half, parts, part_ref, far_ref):
    reads_own = lax.div(lax.axis_index("hist"), rows_dev) == lax.axis_index("col")
    for j, part in enumerate(parts):
        part_ref[j * half : (j + 1) * half, :] = part
        far_ref[j * half : (j + 1) * half, :] = jnp.where(reads_own, 0.0, part)


def first_kernel(rows_dev, half, steps, limits_ref, lesser_hbm, adv_hbm, first_hbm, greater_hbm, coup_hbm, ham_hbm,
                 cur_ref, late_cur_ref, wide_ref, late_wide_ref, active_ref, strength_ref, ham_ref, near_ref, sigma_ref, late_sigma_ref, own_ref,
                 lesser_ref, adv_ref, first_ref, g_ref, h_ref, sems):
    n = 2 * half
    own_row, core, col_pos = places(rows_dev)
    mine, other = core * half, (1 - core) * half
    rows = pl.ds(pl.multiple_of(mine, half), half)
    copies = [
        pltpu.make_async_copy(source, target, sems.at[k])
        for k, (source, target) in enumerate((
            (coup_hbm.at[rows], strength_ref),
            (ham_hbm.at[rows], h_ref),
            (first_hbm, first_ref),
            (greater_hbm.at[pl.ds(0, rows_dev * n)], g_ref),
            (lesser_hbm, lesser_ref),
            (adv_hbm, adv_ref),
        ))
    ]
    for copy in copies:
        copy.start()
    start, cutoff = limits_ref[0:1, :], limits_ref[1:2, :]
    for q in range(steps):
        for s in range(rows_dev):
            active_ref[q * rows_dev + s : q * rows_dev + s + 1, :] = jnp.where(
                col_pos * rows_dev + s < start + q, 1.0, 0.0
            ).astype(F32)
    for copy in copies[:4]:
        copy.wait()
    strength_ref[...] = strength_ref[...] * strength_ref[...]
    ham = h_ref[...]
    ham = tall(jnp.where(core == 0, ham, pltpu.roll(ham, half, 1)))
    ham_ref[...] = ham
    for late, (c_ref, s_ref) in enumerate(((cur_ref, sigma_ref), (late_cur_ref, late_sigma_ref))):
        for p, slot in enumerate(slots(rows_dev, late)):
            c_ref[p] = first_ref[every(mine, jnp.bitwise_xor(own_row, slot), half, rows_dev), :]
        sigmas(0, rows_dev, half, late, c_ref, g_ref, 0, active_ref, strength_ref, s_ref)
    for j in range(2):
        s = jnp.bitwise_xor(own_row, j)
        near_ref[j, :half, :] = first_ref[every(mine, s, half, rows_dev), :]
        near_ref[j, half:, :] = first_ref[every(other, s, half, rows_dev), :]
    for copy in copies[4:]:
        copy.wait()
    split_tables(rows_dev, n, cutoff, lesser_ref, adv_ref, wide_ref, late_wide_ref)
    own_ref[...] = product(sigma_ref[...], wide_ref[...]) + product(late_sigma_ref[...], late_wide_ref[...])


def second_kernel(rows_dev, half, limits_ref, lesser_ref, adv_ref, sigma_ref, late_sigma_ref, own_ref, wide_ref, late_wide_ref, part_ref, far_ref):
    split_tables(rows_dev, 2 * half, limits_ref[1:2, :], lesser_ref, adv_ref, wide_ref, late_wide_ref)
    other = product(sigma_ref[...], wide_ref[...]) + product(late_sigma_ref[...], late_wide_ref[...])
    store(rows_dev, half, (own_ref[...], other), part_ref, far_ref)


def update(prev_ref, pieces, cur_ref, half):
    for k, piece in enumerate(pieces):
        for j in range(2):
            cur_ref[2 * k + j] = prev_ref[2 * k + j] - STEP_SIZE * piece[j * half : (j + 1) * half, :]


def early_kernel(section, rows_dev, half, prev_ref, greater_ref, active_ref, strength_ref, own_wide_ref, other_wide_ref, *rest):
    pieces, (cur_ref, part_ref, sigma_ref) = rest[:2], rest[2:]
    update(prev_ref, pieces, cur_ref, half)
    sigmas(section, rows_dev, half, 0, cur_ref, greater_ref, section * 2 * half, active_ref, strength_ref, sigma_ref)
    part_ref[:half, :] = product(sigma_ref[...], own_wide_ref[...])
    part_ref[half:, :] = product(sigma_ref[...], other_wide_ref[...])


def late_kernel(section, rows_dev, half, prev_ref, greater_ref, active_ref, strength_ref, own_wide_ref, other_wide_ref, early_ref, *rest):
    count = rows_dev // 2 - 2
    pieces, (cur_ref, part_ref, far_ref, sigma_ref) = rest[:count], rest[count:]
    update(prev_ref, pieces, cur_ref, half)
    sigmas(section, rows_dev, half, 1, cur_ref, greater_ref, section * 2 * half, active_ref, strength_ref, sigma_ref)
    parts = [product(sigma_ref[...], table[...]) for table in (own_wide_ref, other_wide_ref)]
    parts = [part + early_ref[j * half : (j + 1) * half, :] for j, part in enumerate(parts)]
    store(rows_dev, half, parts, part_ref, far_ref)


def last_kernel(rows_dev, half, *refs):
    count = rows_dev // 2
    own_row, core, _ = places(rows_dev)
    out_hbm, out_ref, sems = refs[-3:]
    copies = []
    for away in range(2):
        prevs, pieces = refs[2 * away : 2 * away + 2], refs[4 + away * count : 4 + (away + 1) * count]
        side = jnp.bitwise_xor(core, away) * half
        for late, prev_ref in enumerate(prevs):
            for p, slot in enumerate(slots(rows_dev, late)):
                s = jnp.bitwise_xor(own_row, slot ^ away)
                piece = pieces[slot // 2]
                new = prev_ref[p] - STEP_SIZE * piece[slot % 2 * half : (slot % 2 + 1) * half, :]
                out_ref[every(side, s, half, rows_dev), :] = new
        flat = pl.ds(pl.multiple_of(side * rows_dev, half * rows_dev), half * rows_dev)
        copies.append(pltpu.make_async_copy(out_ref.at[flat], out_hbm.at[flat], sems.at[away]))
        copies[-1].start()
    for copy in copies:
        copy.wait()


def call(kernel, ins, outs, scratch, name):
    return pl.pallas_call(
        kernel,
        out_shape=[shape for shape, _ in outs],
        in_specs=[pl.BlockSpec(memory_space=space) for space in ins],
        out_specs=[pl.BlockSpec(memory_space=space) for _, space in outs],
        scratch_shapes=scratch,
        compiler_params=pltpu.CompilerParams(vmem_limit_bytes=VMEM_BYTES),
        name=name,
    )


def in_pairs(hist, lesser, advanced, first_row, greater_rows, hamiltonian, coupling, cutoff, step_index):
    rows_dev, n = lesser.shape[:2]
    steps, half = greater_rows.shape[0], n // 2
    flat = (rows_dev * n, n)
    shape, vmem, hbm = jax.ShapeDtypeStruct, pltpu.VMEM, pltpu.HBM

    def at(h, c):
        return h * 2 + c

    def block(h):
        return h // rows_dev

    def moved(x, pairs):
        return lax.ppermute(x, ("hist", "col"), pairs)

    def flip(x, bits):
        return moved(x, [(at(h, c), at(h ^ bits, c)) for h in range(hist) for c in range(2)])

    cycle = [(at(h, 1 - block(h)), at(h, block(h))) for h in range(hist)]
    cycle += [(at(h, block(h)), at(h ^ rows_dev, block(h))) for h in range(hist)]
    across = [(at(h, 1 - block(h)), at(h ^ rows_dev, block(h))) for h in range(hist)]
    across += [(at(h, block(h)), at(h ^ 1, block(h))) for h in range(hist)]

    def exchange(part, far, turned):
        own = moved(part, cycle) + moved(far, across) + turned
        return [own, flip(own, 1)] + [flip(own, bits) for bits in range(2, rows_dev, 2)]

    def out(dims, kind=F32):
        return shape(dims, kind), vmem

    greater = greater_rows.reshape(steps * rows_dev * n, n)
    tables = lesser.reshape(flat), advanced.reshape(flat)
    limits = jnp.broadcast_to(jnp.concatenate([step_index, cutoff])[:, None], (2, n))
    near_out = out((2, n, n))
    few, rest = 4, rows_dev - 4
    cur_outs = [out((count, half, n)) for count in (few, rest)]
    wide_outs = [out((2 * count * n, 2 * n), BF16) for count in (few, rest)]
    sigma_outs = [out((n, 2 * count * n), BF16) for count in (few, rest)]
    pair_out = out((n, n))
    *currents, own_wide, own_late_wide, active, strength, ham, near, sigma, late_sigma, own_part = call(
        functools.partial(first_kernel, rows_dev, half, steps),
        [vmem] + [hbm] * 6,
        [*cur_outs, *wide_outs, out((steps * rows_dev, n)), out((half, n)), out((n, n), BF16), near_out, *sigma_outs, out((half, n))],
        [vmem(flat, F32)] * 4 + [vmem((half, n), F32), pltpu.SemaphoreType.DMA((6,))],
        "first_step",
    )(limits, *[
        pltpu.with_memory_space_constraint(x, hbm)
        for x in (*tables, first_row.reshape(flat), greater, coupling, hamiltonian)
    ])
    other_wide, other_late_wide, part, far = call(
        functools.partial(second_kernel, rows_dev, half),
        [vmem] * 6, [*wide_outs, pair_out, pair_out], [], "first_step_other",
    )(flip(limits, 1), *[flip(x, 1) for x in tables], sigma, late_sigma, own_part)
    swap = []
    for section in range(1, steps + 1):
        last = section == steps and len(swap) == 2
        *new, turned = call(
            functools.partial(turn_last, half) if last else functools.partial(turn, half, len(swap)),
            [vmem] * (4 + len(swap)),
            [near_out] * (0 if last else len(swap) // 2) + [pair_out],
            [vmem((2, n, n), F32)] if last else [],
            "turn",
        )(ham, near, part, far, *swap)
        near = new[0] if new else near
        own, swapped, *others = exchange(part, far, turned)
        swap = [own, swapped]
        if section == steps:
            break
        given = greater, active, strength
        early, part = call(
            functools.partial(early_kernel, section, rows_dev, half),
            [vmem] * 8, [cur_outs[0], pair_out], [vmem(*x) for x in [((n, 2 * few * n), BF16)]], "next_step_early",
        )(currents[0], *given, own_wide, other_wide, own, others[-1])
        late, part, far = call(
            functools.partial(late_kernel, section, rows_dev, half),
            [vmem] * (7 + len(others) - 1), [cur_outs[1], pair_out, pair_out], [vmem((n, 2 * rest * n), BF16)], "next_step",
        )(currents[1], *given, own_late_wide, other_late_wide, part, *others[:-1])
        currents = [early, late]
    pieces = [own] + others
    final = call(
        functools.partial(last_kernel, rows_dev, half),
        [vmem] * (4 + rows_dev), [(shape(flat, F32), hbm)], [vmem(flat, F32), pltpu.SemaphoreType.DMA((2,))], "last_step",
    )(*currents, *[flip(x, 1) for x in currents], *pieces, swapped, *[flip(x, 1) for x in others])[0]
    return final.reshape(first_row.shape)


def in_general(lesser, advanced, first_row, greater_rows, hamiltonian, coupling, cutoff, step_index):
    rows_dev, orbitals, cols_dev, _ = lesser.shape
    row_times = lax.axis_index("col") * rows_dev + jnp.arange(rows_dev, dtype=jnp.int32)
    inside = (row_times[:, None] < cutoff[None, :]).astype(F32)
    adv_flat = (advanced * inside[:, None, :, None]).reshape(rows_dev * orbitals, cols_dev * orbitals)
    hist_flat = lesser.reshape(rows_dev * orbitals, cols_dev * orbitals)
    propagator = jnp.eye(orbitals, dtype=F32) - STEP_SIZE * hamiltonian
    strength = (coupling * coupling)[:, None, :]
    current = first_row
    for section in range(greater_rows.shape[0]):
        greater = greater_rows[section]
        sigma_less = -strength * current * current * greater
        sigma_ret = -strength * greater * greater * current - sigma_less
        active = (row_times < step_index[0] + section).astype(F32)
        ret_flat = (sigma_ret * active[None, :, None]).reshape(orbitals, rows_dev * orbitals)
        less_flat = sigma_less.reshape(orbitals, rows_dev * orbitals)
        memory = jnp.dot(ret_flat, hist_flat, precision=PRECISE, preferred_element_type=F32)
        memory = memory + jnp.dot(less_flat, adv_flat, precision=PRECISE, preferred_element_type=F32)
        share = lax.psum_scatter(memory.reshape(orbitals, cols_dev, orbitals), "col", scatter_dimension=0, tiled=True)
        spread = lax.all_gather(share, "hist", axis=1, tiled=True)
        memory_block = lax.all_to_all(spread, "col", split_axis=1, concat_axis=0, tiled=True)
        moved = jnp.einsum("ik,ksj->isj", propagator, current, precision=PRECISE)
        current = moved - STEP_SIZE * memory_block
    return current


def solution(mesh):
    hist, cols = mesh.shape["hist"], mesh.shape["col"]

    def on_device(lesser, *rest):
        rows_dev, _, cols_dev, _ = lesser.shape
        if cols == 2 and cols_dev == 1 and hist == 2 * rows_dev and hist & (hist - 1) == 0 and rows_dev > 4:
            return in_pairs(hist, lesser, *rest)
        return in_general(lesser, *rest)

    in_specs = (
        P("col", None, "hist", None),
        P("col", None, "hist", None),
        P(None, "col", None),
        P(None, None, "col", None),
        P(),
        P(),
        P("hist"),
        P(),
    )
    return jax.shard_map(on_device, mesh=mesh, in_specs=in_specs, out_specs=P(None, "col", None), check_vma=False)
```
